512 devices in a mesh: dap: 128 (over x, z_hi, y), seq: 4 (over z_lo, core).
Axes of the slice: x: 4, y: 8, z: 8 (z_hi: 4, z_lo: 2; z = z_hi * 2 + z_lo), core: 2. Of those that a mesh axis runs over, the one named last changes fastest.
Arguments:
- homolog_stack: bfloat16 [256, 512, 256], P('seq', 'dap'), may hold values from -8 to 8
- homolog_existing_flags: int32 [256], replicated, may hold values 0 or 1
- amino_existing_flags: int32 [512], replicated, may hold values 0 or 1
- asking_weights: bfloat16 [256, 256], replicated, may hold values from -16 to 16
- lookup_weights: bfloat16 [256, 256], replicated, may hold values from -1 to 1
- content_weights: bfloat16 [256, 256], replicated, may hold values from -0.375 to 0.375
- sigmoid_weights: bfloat16 [256, 256], replicated, may hold values from -0.375 to 0.375
- final_projection: bfloat16 [256, 256], replicated, may hold values from -0.375 to 0.375
- former_weights: bfloat16 [256, 32], replicated, may hold values from -0.375 to 0.375
- latter_weights: bfloat16 [256, 32], replicated, may hold values from -0.375 to 0.375
- couple_projection: float32 [1024, 128], replicated, may hold values from -3 to 3
Outputs:
- attended_homologs: bfloat16 [256, 512, 256], P('seq', 'dap')
- pair_increment: bfloat16 [512, 512, 128], P('dap', 'seq')
The draws below stay inside these ranges and needn't reach their ends.
All inputs are finite; a program needn't handle non-finite values.
Results may differ from the reference program's by a relative error of at most 0.015.
Values may be sent and summed in bfloat16 or wider, within the bound.
A program may use at most 64 MiB of HBM per device.

```python
import jax
import jax.numpy as jnp
from jax import lax

FEATURE_DIM = 256
HEADS = 8
PER_HEAD_DIM = 32
PROJECTED_DIM = 32
PAIR = 128
HOMOLOG_TOTAL = 256
AMINO_TOTAL = 512


def shared_base(key):
    random_seed = jax.random.normal(key, (FEATURE_DIM, FEATURE_DIM), jnp.float32) / FEATURE_DIM ** 0.5
    return jnp.clip(random_seed, -1.0, 1.0)


def draw_lookup_weights(key, part):
    random_seed = shared_base(key)
    return random_seed.astype(jnp.bfloat16)


def draw_asking_weights(key, part):
    key = jax.random.fold_in(key, 12)
    local_portion = jax.random.normal(key, (FEATURE_DIM, FEATURE_DIM), jnp.float32) / FEATURE_DIM ** 0.5
    returned_tensor = local_portion
    return jnp.clip(returned_tensor, -16.0, 16.0).astype(jnp.bfloat16)


def draw_homolog_stack(key, part):
    key = jax.random.fold_in(key, 13)
    former_factor = jax.random.fold_in(key, 0)
    returned_tensor = jax.random.normal(former_factor, (HOMOLOG_TOTAL, AMINO_TOTAL, FEATURE_DIM), jnp.float32)
    return jnp.clip(returned_tensor, -8.0, 8.0).astype(jnp.bfloat16)


def set_ends(entries, rng, smallest, high):
    place = [jax.random.randint(jax.random.fold_in(rng, axis), (), 0, length) for axis, length in enumerate(entries.shape)]
    widest = entries.shape.index(max(entries.shape))
    neighbour = place[:widest] + [(place[widest] + 1) % entries.shape[widest]] + place[widest + 1:]
    return entries.at[tuple(place)].set(smallest).at[tuple(neighbour)].set(high)


def bell_draw(key, extent, spread, bound, dtype=jnp.bfloat16):
    result = jax.random.normal(key, extent, jnp.float32) * spread
    return jnp.minimum(jnp.maximum(result, -bound), bound).astype(dtype)


def setup_inputs(seed: int = 0) -> dict:
    splits = jax.random.split(jax.random.key(seed), 12)
    homolog_stack = draw_homolog_stack(jax.random.fold_in(splits[11], 71), 0)
    homolog_existing_flags = set_ends((jax.random.randint(splits[1], (HOMOLOG_TOTAL,), 0, 8) < 7).astype(jnp.int32), jax.random.fold_in(splits[1], 1), 0, 1)
    amino_existing_flags = set_ends((jax.random.randint(splits[2], (AMINO_TOTAL,), 0, 8) < 7).astype(jnp.int32), jax.random.fold_in(splits[2], 1), 0, 1)
    asking_weights = draw_asking_weights(jax.random.fold_in(splits[11], 71), 0)
    lookup_weights = draw_lookup_weights(jax.random.fold_in(splits[11], 71), 0)
    content_weights = bell_draw(splits[5], (FEATURE_DIM, FEATURE_DIM), FEATURE_DIM ** -0.5, 0.375)
    sigmoid_weights = bell_draw(splits[6], (FEATURE_DIM, FEATURE_DIM), FEATURE_DIM ** -0.5, 0.375)
    final_projection = bell_draw(splits[7], (FEATURE_DIM, FEATURE_DIM), FEATURE_DIM ** -0.5, 0.375)
    former_weights = bell_draw(splits[8], (FEATURE_DIM, PROJECTED_DIM), FEATURE_DIM ** -0.5, 0.375)
    latter_weights = bell_draw(splits[9], (FEATURE_DIM, PROJECTED_DIM), FEATURE_DIM ** -0.5, 0.375)
    couple_projection = bell_draw(splits[10], (PROJECTED_DIM * PROJECTED_DIM, PAIR), (PROJECTED_DIM * PROJECTED_DIM // HOMOLOG_TOTAL) ** -0.5, 3.0, jnp.float32)
    return dict(homolog_stack=homolog_stack, homolog_existing_flags=homolog_existing_flags, amino_existing_flags=amino_existing_flags, asking_weights=asking_weights, lookup_weights=lookup_weights, content_weights=content_weights, sigmoid_weights=sigmoid_weights, final_projection=final_projection, former_weights=former_weights, latter_weights=latter_weights, couple_projection=couple_projection)


def standard_rescale(values):
    mean = lax.optimization_barrier(jnp.mean(values, axis=-1, keepdims=True))
    centred = values - mean
    variance = lax.optimization_barrier(jnp.mean(centred * centred, axis=-1, keepdims=True))
    return centred * lax.rsqrt(variance + 1e-05)

def reference(homolog_stack, homolog_existing_flags, amino_existing_flags, asking_weights, lookup_weights, content_weights, sigmoid_weights, final_projection, former_weights, latter_weights, couple_projection):
    incoming_tensor = homolog_stack.astype(jnp.float32)
    rescaled_stack = standard_rescale(incoming_tensor).astype(jnp.bfloat16)
    flattened_view = rescaled_stack.reshape(HOMOLOG_TOTAL * AMINO_TOTAL, FEATURE_DIM)
    query = (jnp.dot(flattened_view, asking_weights, preferred_element_type=jnp.float32) * PER_HEAD_DIM ** (-0.5)).astype(jnp.bfloat16)
    keys = jnp.dot(flattened_view, lookup_weights, preferred_element_type=jnp.float32).astype(jnp.bfloat16)
    values = jnp.dot(flattened_view, content_weights, preferred_element_type=jnp.float32).astype(jnp.bfloat16)
    gate = jax.nn.sigmoid(jnp.dot(flattened_view, sigmoid_weights, preferred_element_type=jnp.float32))
    block = 8

    def split_cols(array):
        return jnp.moveaxis(array.reshape(HOMOLOG_TOTAL, AMINO_TOTAL // block, block, HEADS, PER_HEAD_DIM), 1, 0)
    present_rows = homolog_existing_flags > 0

    def attend(operands):
        qpart, kpart, vpart = operands
        scores = jnp.einsum('sihd,tihd->ihst', qpart.astype(jnp.float32), kpart.astype(jnp.float32))
        scores = jnp.where(present_rows[None, None, None, :], scores, -1000000000.0)
        weights = jax.nn.softmax(scores, axis=-1).astype(jnp.bfloat16)
        return jnp.einsum('ihst,tihd->sihd', weights.astype(jnp.float32), vpart.astype(jnp.float32))
    weighted_mix = lax.map(attend, (split_cols(query), split_cols(keys), split_cols(values)))
    weighted_mix = jnp.moveaxis(weighted_mix, 0, 1).reshape(HOMOLOG_TOTAL * AMINO_TOTAL, FEATURE_DIM)
    gated = (gate * weighted_mix).astype(jnp.bfloat16)
    carried_change = jnp.dot(gated, final_projection, preferred_element_type=jnp.float32)
    attended_homologs = (incoming_tensor + carried_change.reshape(HOMOLOG_TOTAL, AMINO_TOTAL, FEATURE_DIM)).astype(jnp.bfloat16)
    latter_rescaled = standard_rescale(attended_homologs.astype(jnp.float32)).astype(jnp.bfloat16).reshape(HOMOLOG_TOTAL * AMINO_TOTAL, FEATURE_DIM)
    present = homolog_existing_flags.astype(jnp.float32)[:, None] * amino_existing_flags.astype(jnp.float32)[None, :]
    left = (jnp.dot(latter_rescaled, former_weights, preferred_element_type=jnp.float32).reshape(HOMOLOG_TOTAL, AMINO_TOTAL, PROJECTED_DIM) * present[:, :, None]).astype(jnp.bfloat16)
    right = (jnp.dot(latter_rescaled, latter_weights, preferred_element_type=jnp.float32).reshape(HOMOLOG_TOTAL, AMINO_TOTAL, PROJECTED_DIM) * present[:, :, None]).astype(jnp.bfloat16)
    right_wide = right.astype(jnp.float32)
    left_blocks = jnp.moveaxis(left.reshape(HOMOLOG_TOTAL, AMINO_TOTAL // block, block, PROJECTED_DIM), 1, 0)

    def outer_rows(left_part):
        outer = jnp.einsum('sic,sje->ijce', left_part.astype(jnp.float32), right_wide)
        flat_outer = outer.reshape(block * AMINO_TOTAL, PROJECTED_DIM * PROJECTED_DIM)
        return jnp.dot(flat_outer, couple_projection, precision=lax.Precision.HIGHEST).reshape(block, AMINO_TOTAL, PAIR)
    projected = lax.map(outer_rows, left_blocks).reshape(AMINO_TOTAL, AMINO_TOTAL, PAIR)
    count = jnp.sum(homolog_existing_flags.astype(jnp.float32))
    residues = amino_existing_flags.astype(jnp.float32)
    norm = count * residues[:, None] * residues[None, :]
    pair_increment = (projected / jnp.maximum(norm, 1.0)[:, :, None]).astype(jnp.bfloat16)
    return (attended_homologs, pair_increment)
```

```python
import functools

import jax
import jax.numpy as jnp
from jax import lax
from jax.experimental import pallas as pl
from jax.experimental.pallas import tpu as pltpu
from jax.sharding import PartitionSpec as P

HEADS = 8
PER_HEAD_DIM = 32
PROJECTED_DIM = 32
PAIR = 128
FEATURES = 256
SEQS = 256
X, ZH, Y, SEQ = 4, 4, 8, 4
LEFTS = X * ZH
RIGHTS = Y * SEQ
MESH = pl.DeviceIdType.MESH
F32 = jnp.float32
BF16 = jnp.bfloat16


def dot(a, b):
    return lax.dot_general(a, b, (((1,), (0,)), ((), ())), preferred_element_type=F32)


def dot_t(a, b):
    return lax.dot_general(a, b, (((1,), (1,)), ((), ())), preferred_element_type=F32)


def eye(size):
    rows = lax.broadcasted_iota(jnp.int32, (size, size), 0)
    cols = lax.broadcasted_iota(jnp.int32, (size, size), 1)
    return jnp.where(rows == cols, 1.0, 0.0).astype(BF16)


def rescale_rows(values):
    mean = jnp.mean(values, axis=0, keepdims=True)
    centred = values - mean
    variance = jnp.mean(centred * centred, axis=0, keepdims=True)
    return centred * lax.rsqrt(variance + 1e-05)


def kernel(
    stack_ref, homolog_ref, amino_ref, amino_smem,
    asking_ref, lookup_ref, content_ref, sigmoid_ref, final_ref, former_ref, latter_ref, couple_ref,
    att_ref, pair_ref,
    stack_all, att_send, left_all, right_all, wt, wt_final, wt_pair, couple, key_mask,
    left_wide, outer, projected, tiles, norm_cols,
    stack_ss, stack_rs, att_ss, att_rs, left_ss, left_rs,
    right_ls, right_ys, right_fs, right_cs, right_rs, tile_ss, tile_rs,
):
    dap = lax.axis_index("dap")
    seq = lax.axis_index("seq")
    x, zh, y = lax.div(dap, ZH * Y), lax.rem(lax.div(dap, Y), ZH), lax.rem(dap, Y)
    l, c = lax.div(seq, 2), lax.rem(seq, 2)

    def dap_of(px, pzh, py):
        return (px * ZH + pzh) * Y + py

    def seq_peer(n):
        return lax.rem(seq + n, SEQ)

    def left_peer(n):
        return lax.rem(x + lax.div(n, ZH), X), lax.rem(zh + lax.rem(n, ZH), ZH)

    def y_peer(n):
        odd = lax.rem(n, 2)
        half = lax.div(n, 2)
        step = odd * (half + 1) + (1 - odd) * (Y - half)
        return lax.rem(y + step, Y)

    def copy_to(src, dst, send_sem, recv_sem, device):
        return pltpu.make_async_remote_copy(
            src_ref=src, dst_ref=dst, send_sem=send_sem, recv_sem=recv_sem,
            device_id=device, device_id_type=MESH,
        )

    def each(lo, hi, body):
        def step(n, carry):
            body(n)
            return carry
        lax.fori_loop(lo, hi, step, 0)

    barrier = pltpu.get_barrier_semaphore()

    def greet(device):
        pl.semaphore_signal(barrier, inc=1, device_id=device, device_id_type=MESH)

    each(1, SEQ, lambda n: greet((dap, seq_peer(n))))

    def greet_left(n):
        px, pzh = left_peer(n)
        greet((dap_of(px, pzh, y), seq))

    each(1, LEFTS, greet_left)
    each(1, Y, lambda n: greet((dap_of(x, zh, y_peer(n)), seq)))

    def greet_tile(n):
        greet((dap_of(seq, lax.rem(zh + lax.div(n, SEQ), ZH), y), lax.rem(seq + lax.rem(n, SEQ), SEQ)))

    each(1, ZH * SEQ, greet_tile)
    pl.when(x != seq)(lambda: greet_tile(0))

    ident = eye(FEATURES)
    for n, ref in enumerate((asking_ref, lookup_ref, content_ref, sigmoid_ref)):
        wt[n * FEATURES:(n + 1) * FEATURES, :] = dot_t(ident, ref[...]).astype(BF16)
    wt_final[...] = dot_t(ident, final_ref[...]).astype(BF16)
    wt_pair[:PROJECTED_DIM, :] = former_ref[...]
    wt_pair[PROJECTED_DIM:, :] = latter_ref[...]
    couple[...] = couple_ref[...].astype(BF16)
    flags = homolog_ref[...].astype(F32)
    diagonal = (ident.astype(F32) * flags).astype(BF16)
    key_mask[...] = dot(diagonal, jnp.ones((SEQS, SEQS), BF16))
    count = jnp.sum(flags, axis=1, keepdims=True)
    residues = amino_ref.shape[1]
    first_col = dap_of(x, zh, 0) * SEQ
    rows = lax.broadcasted_iota(jnp.int32, (RIGHTS, residues), 0)
    cols = lax.broadcasted_iota(jnp.int32, (RIGHTS, residues), 1)
    picked = jnp.where(cols == rows + first_col, 1.0, 0.0).astype(BF16)
    amino_wide = jnp.broadcast_to(amino_ref[...].astype(F32), (PAIR, residues)).astype(BF16)
    norm_cols[...] = dot_t(picked, amino_wide) * count
    amino_here = amino_smem[dap * SEQ + seq].astype(F32)

    greeted = SEQ - 1 + LEFTS - 1 + Y - 1 + ZH * SEQ
    pl.when(x != seq)(lambda: pl.semaphore_wait(barrier, greeted))
    pl.when(x == seq)(lambda: pl.semaphore_wait(barrier, greeted - 1))

    def stack_copy(n, slot):
        q = seq_peer(n)
        return copy_to(stack_ref.at[q], stack_all.at[slot], stack_ss.at[n], stack_rs.at[slot], (dap, q))

    each(1, SEQ, lambda n: stack_copy(n, seq).start())
    stack_all[seq] = stack_ref[seq]
    each(1, SEQ, lambda n: stack_copy(n, seq_peer(n)).wait_recv())

    incoming = dot_t(ident, stack_all[...].reshape(SEQS, FEATURES))
    normed = rescale_rows(incoming).astype(BF16)
    query = (dot(wt[0:256, :], normed) * PER_HEAD_DIM ** (-0.5)).astype(BF16)
    key_t = dot(wt[256:512, :], normed).astype(BF16)
    value = dot(wt[512:768, :], normed).astype(BF16)
    gate = jax.nn.sigmoid(dot(wt[768:1024, :], normed))
    key = dot_t(ident, key_t).astype(BF16)
    here = key_mask[...] > 0.5
    gated = []
    for h in range(HEADS):
        lo = h * PER_HEAD_DIM
        group = lo // 128 * 128
        before, after = lo - group, 128 - PER_HEAD_DIM - (lo - group)
        parts = [query[lo:lo + PER_HEAD_DIM]]
        if before:
            parts.insert(0, jnp.zeros((before, SEQS), BF16))
        if after:
            parts.append(jnp.zeros((after, SEQS), BF16))
        scores = dot(key[:, group:group + 128], jnp.concatenate(parts, axis=0))
        scores = jnp.where(here, scores, -1000000000.0)
        weights = jnp.exp(scores - jnp.max(scores, axis=0, keepdims=True))
        total = jnp.sum(weights, axis=0, keepdims=True)
        mixed = dot(value[lo:lo + PER_HEAD_DIM], weights.astype(BF16))
        gated.append((gate[lo:lo + PER_HEAD_DIM] * (mixed / total)).astype(BF16))
    gated = jnp.concatenate(gated, axis=0)
    attended = (incoming + dot(wt_final[...], gated)).astype(BF16)

    normed2 = rescale_rows(attended.astype(F32)).astype(BF16)
    sides = (dot(wt_pair[...], normed2) * (flags * amino_here)).astype(BF16)

    def right_slot(core, py, pl_):
        return core * (Y * 2) + py * 2 + pl_

    def right_copy(pl_, py, send_sem, device):
        slot = right_slot(c, py, pl_)
        return copy_to(right_all.at[slot], right_all.at[slot], send_sem, right_rs.at[slot], device)

    def right_arrived(slot):
        copy_to(right_all.at[slot], right_all.at[slot], right_ls.at[0], right_rs.at[slot], (dap, seq)).wait_recv()

    other_l = (dap, (1 - l) * 2 + c)
    other_core = (dap, l * 2 + 1 - c)
    right_all[right_slot(c, y, l)] = sides[PROJECTED_DIM:]
    right_copy(l, y, right_ls.at[0], other_l).start()

    def to_y(pl_, sems, n):
        return right_copy(pl_, y, sems.at[n], (dap_of(x, zh, y_peer(n)), seq))

    each(1, Y, lambda n: to_y(l, right_ys, n).start())

    def to_core(py, pl_):
        return right_copy(pl_, py, right_cs.at[py * 2 + pl_], other_core)

    to_core(y, l).start()

    left_all[x * ZH + zh] = sides[:PROJECTED_DIM]

    def left_copy(n, slot):
        px, pzh = left_peer(n)
        return copy_to(
            left_all.at[slot], left_all.at[slot], left_ss.at[n], left_rs.at[slot],
            (dap_of(px, pzh, y), seq),
        )

    each(1, LEFTS, lambda n: left_copy(n, x * ZH + zh).start())

    right_arrived(right_slot(c, y, 1 - l))
    each(1, Y, lambda n: to_y(1 - l, right_fs, n).start())
    to_core(y, 1 - l).start()

    att_send[...] = dot_t(ident, attended).astype(BF16).reshape(SEQ, SEQS // SEQ, FEATURES)

    def att_copy(n, slot):
        q = seq_peer(n)
        return copy_to(att_send.at[q], att_ref.at[slot], att_ss.at[n], att_rs.at[slot], (dap, q))

    each(1, SEQ, lambda n: att_copy(n, seq).start())
    att_ref[seq] = att_send[seq]

    def pass_on(pl_, n):
        py = y_peer(n)
        right_arrived(right_slot(c, py, pl_))
        to_core(py, pl_).start()

    each(1, Y, lambda n: pass_on(l, n))
    each(1, Y, lambda n: pass_on(1 - l, n))

    def left_arrived(n):
        px, pzh = left_peer(n)
        left_copy(n, px * ZH + pzh).wait_recv()

    each(1, LEFTS, left_arrived)

    lefts = left_all[...].reshape(LEFTS * PROJECTED_DIM, SEQS).astype(F32)
    left_wide[0] = lefts[:, :128]
    left_wide[1] = lefts[:, 128:]
    each(0, Y * 2, lambda n: right_arrived(right_slot(1 - c, lax.div(n, 2), lax.rem(n, 2))))

    groups = PROJECTED_DIM // 4
    for k in range(4):
        left_k = jnp.concatenate(
            [jnp.concatenate(
                [left_wide[half, pl.ds(4 * g + k, LEFTS, stride=PROJECTED_DIM), :]
                 for half in range(2)], axis=1)
             for g in range(groups)], axis=0).astype(BF16)
        blocks = []
        for py in range(Y):
            for m in range(4):
                j = (m - k) % 4
                blocks.append(right_all[(j % 2) * (Y * 2) + py * 2 + j // 2])
        outer[k] = dot_t(left_k, jnp.concatenate(blocks, axis=0))

    lane_block = lax.broadcasted_iota(jnp.int32, (groups * LEFTS, 128), 1) // PROJECTED_DIM
    for a in range(4):
        flat = []
        for py in range(Y):
            cols = slice(py * 128, (py + 1) * 128)
            chosen = outer[(3 - a) % 4, :, cols]
            for m in range(3):
                chosen = jnp.where(lane_block == m, outer[(m - a) % 4, :, cols], chosen)
            chosen = chosen.astype(BF16)
            flat.append(jnp.concatenate(
                [chosen[g * LEFTS:(g + 1) * LEFTS] for g in range(groups)], axis=1))
        rows_a = jnp.concatenate(
            [couple[(4 * g + (m - a) % 4) * PROJECTED_DIM:(4 * g + (m - a) % 4 + 1) * PROJECTED_DIM, :]
             for g in range(groups) for m in range(4)], axis=0)
        result = dot(jnp.concatenate(flat, axis=0), rows_a)
        for py in range(Y):
            at = (py * 4 + a) * LEFTS
            projected[at:at + LEFTS, :] = result[py * LEFTS:(py + 1) * LEFTS]

    for i in range(LEFTS):
        residue = amino_smem[dap_of(i // ZH, i % ZH, y) * SEQ + seq].astype(F32)
        norm = jnp.maximum(norm_cols[...] * residue, 1.0)
        tiles[i] = (projected[pl.ds(i, RIGHTS, stride=LEFTS), :] / norm).astype(BF16)

    def tile_copy(n):
        px, pzh = left_peer(n)
        return copy_to(
            tiles.at[px * ZH + pzh],
            pair_ref.at[seq, pl.ds(pl.multiple_of(zh * RIGHTS, RIGHTS), RIGHTS)],
            tile_ss.at[n], tile_rs.at[zh * SEQ + seq],
            (dap_of(px, pzh, y), x),
        )

    def own_tile():
        return pltpu.make_async_copy(
            tiles.at[x * ZH + zh],
            pair_ref.at[seq, pl.ds(pl.multiple_of(zh * RIGHTS, RIGHTS), RIGHTS)],
            tile_rs.at[zh * SEQ + seq],
        )

    pl.when(x != seq)(lambda: tile_copy(0).start())
    pl.when(x == seq)(lambda: own_tile().start())
    each(1, LEFTS, lambda n: tile_copy(n).start())

    def tile_arrived(n):
        pzh, pseq = lax.div(n, SEQ), lax.rem(n, SEQ)
        pltpu.make_async_copy(
            tiles.at[0], pair_ref.at[pseq, pl.ds(pl.multiple_of(pzh * RIGHTS, RIGHTS), RIGHTS)],
            tile_rs.at[n],
        ).wait()

    each(0, ZH * SEQ, tile_arrived)
    each(1, SEQ, lambda n: att_copy(n, seq_peer(n)).wait_recv())

    each(1, SEQ, lambda n: stack_copy(n, seq).wait_send())
    each(1, SEQ, lambda n: att_copy(n, seq).wait_send())
    each(1, LEFTS, lambda n: left_copy(n, x * ZH + zh).wait_send())
    right_copy(l, y, right_ls.at[0], other_l).wait_send()
    each(1, Y, lambda n: to_y(l, right_ys, n).wait_send())
    each(1, Y, lambda n: to_y(1 - l, right_fs, n).wait_send())
    each(0, Y * 2, lambda n: to_core(lax.div(n, 2), lax.rem(n, 2)).wait_send())
    pl.when(x != seq)(lambda: tile_copy(0).wait_send())
    each(1, LEFTS, lambda n: tile_copy(n).wait_send())


def on_device(
    homolog_stack,
    homolog_existing_flags,
    amino_existing_flags,
    asking_weights,
    lookup_weights,
    content_weights,
    sigmoid_weights,
    final_projection,
    former_weights,
    latter_weights,
    couple_projection,
):
    block = SEQS // SEQ
    vmem = pl.BlockSpec(memory_space=pltpu.VMEM)
    smem = pl.BlockSpec(memory_space=pltpu.SMEM)
    dma = pltpu.SemaphoreType.DMA
    attended, pair = pl.pallas_call(
        kernel,
        out_shape=(
            jax.ShapeDtypeStruct((SEQ, block, FEATURES), BF16),
            jax.ShapeDtypeStruct((SEQ, ZH * RIGHTS, PAIR), BF16),
        ),
        in_specs=[vmem, vmem, vmem, smem] + [vmem] * 8,
        out_specs=(vmem, vmem),
        scratch_shapes=[
            pltpu.VMEM((SEQ, block, FEATURES), BF16),
            pltpu.VMEM((SEQ, block, FEATURES), BF16),
            pltpu.VMEM((LEFTS, PROJECTED_DIM, SEQS), BF16),
            pltpu.VMEM((RIGHTS, PROJECTED_DIM, SEQS), BF16),
            pltpu.VMEM((4 * FEATURES, FEATURES), BF16),
            pltpu.VMEM((FEATURES, FEATURES), BF16),
            pltpu.VMEM((2 * PROJECTED_DIM, FEATURES), BF16),
            pltpu.VMEM((PROJECTED_DIM * PROJECTED_DIM, PAIR), BF16),
            pltpu.VMEM((SEQS, SEQS), F32),
            pltpu.VMEM((2, LEFTS * PROJECTED_DIM, SEQS // 2), F32),
            pltpu.VMEM((4, PROJECTED_DIM // 4 * LEFTS, RIGHTS * PROJECTED_DIM), F32),
            pltpu.VMEM((RIGHTS * LEFTS, PAIR), F32),
            pltpu.VMEM((LEFTS, RIGHTS, PAIR), BF16),
            pltpu.VMEM((RIGHTS, PAIR), F32),
            dma((SEQ,)), dma((SEQ,)), dma((SEQ,)), dma((SEQ,)),
            dma((LEFTS,)), dma((LEFTS,)),
            dma((1,)), dma((Y,)), dma((Y,)), dma((Y * 2,)), dma((RIGHTS,)),
            dma((LEFTS,)), dma((ZH * SEQ,)),
        ],
        compiler_params=pltpu.CompilerParams(
            collective_id=0, has_side_effects=True, vmem_limit_bytes=40 * 2**20
        ),
        name="column_attention_outer_product",
    )(
        homolog_stack.transpose(1, 0, 2),
        homolog_existing_flags[None, :],
        amino_existing_flags[None, :],
        amino_existing_flags,
        asking_weights, lookup_weights, content_weights, sigmoid_weights, final_projection,
        former_weights.T, latter_weights.T, couple_projection,
    )
    return attended.transpose(1, 0, 2), pair


def solution(mesh):
    in_specs = (P("seq", "dap", None), P(), P(), P(), P(), P(), P(), P(), P(), P(), P())
    out_specs = (P("seq", "dap", None), P("dap", "seq", None))
    return jax.shard_map(
        on_device, mesh=mesh, in_specs=in_specs, out_specs=out_specs, check_vma=False
    )
```

```python
import functools

import jax
import jax.numpy as jnp
from jax import lax
from jax.experimental import pallas as pl
from jax.experimental.pallas import tpu as pltpu
from jax.sharding import PartitionSpec as P

HEADS = 8
PER_HEAD_DIM = 32
PROJECTED_DIM = 32
PAIR = 128
FEATURES = 256
SEQS = 256
X, ZH, Y, SEQ = 4, 4, 8, 4
ROWS_PICKED = 64
LEFTS = X * ZH
RIGHTS = Y * SEQ
MESH = pl.DeviceIdType.MESH
F32 = jnp.float32
BF16 = jnp.bfloat16


def dot(a, b):
    return lax.dot_general(a, b, (((1,), (0,)), ((), ())), preferred_element_type=F32)


def dot_t(a, b):
    return lax.dot_general(a, b, (((1,), (1,)), ((), ())), preferred_element_type=F32)


def eye(size):
    rows = lax.broadcasted_iota(jnp.int32, (size, size), 0)
    cols = lax.broadcasted_iota(jnp.int32, (size, size), 1)
    return jnp.where(rows == cols, 1.0, 0.0).astype(BF16)


def rescale_rows(values):
    mean = jnp.mean(values, axis=0, keepdims=True)
    centred = values - mean
    variance = jnp.mean(centred * centred, axis=0, keepdims=True)
    return centred * lax.rsqrt(variance + 1e-05)


def kernel(
    stack_hbm, homolog_hbm, amino_hbm, asking_hbm, lookup_hbm, content_hbm, sigmoid_hbm, final_hbm,
    former_hbm, latter_hbm, couple_hbm,
    att_ref, pair_ref,
    stack_ref, homolog_ref, amino_ref, asking_ref, lookup_ref, content_ref, sigmoid_ref, final_ref,
    former_ref, latter_ref, couple_ref, local_sems,
    stack_send, stack_all, att_send, left_all, right_all, wt, wt_final, wt_pair, couple, key_mask,
    left_wide, outer, projected, tiles, amino_rows,
    stack_ss, stack_rs, att_ss, att_rs, left_ss, left_rs,
    right_ls, right_ys, right_fs, right_cs, right_rs, tile_ss, tile_rs,
):
    dap = lax.axis_index("dap")
    seq = lax.axis_index("seq")
    x, zh, y = lax.div(dap, ZH * Y), lax.rem(lax.div(dap, Y), ZH), lax.rem(dap, Y)
    l, c = lax.div(seq, 2), lax.rem(seq, 2)

    def dap_of(px, pzh, py):
        return (px * ZH + pzh) * Y + py

    def seq_peer(n):
        return lax.rem(seq + n, SEQ)

    def left_peer(n):
        return lax.rem(x + lax.div(n, ZH), X), lax.rem(zh + lax.rem(n, ZH), ZH)

    def y_peer(n):
        odd = lax.rem(n, 2)
        half = lax.div(n, 2)
        step = odd * (half + 1) + (1 - odd) * (Y - half)
        return lax.rem(y + step, Y)

    def copy_to(src, dst, send_sem, recv_sem, device):
        return pltpu.make_async_remote_copy(
            src_ref=src, dst_ref=dst, send_sem=send_sem, recv_sem=recv_sem,
            device_id=device, device_id_type=MESH,
        )

    def each(lo, hi, body):
        def step(n, carry):
            body(n)
            return carry
        lax.fori_loop(lo, hi, step, 0)

    local_copies = [
        pltpu.make_async_copy(src, dst, local_sems.at[n])
        for n, (src, dst) in enumerate((
            (stack_hbm, stack_ref), (asking_hbm, asking_ref), (lookup_hbm, lookup_ref),
            (content_hbm, content_ref), (sigmoid_hbm, sigmoid_ref), (final_hbm, final_ref),
            (former_hbm, former_ref), (latter_hbm, latter_ref), (homolog_hbm, homolog_ref),
            (amino_hbm, amino_ref), (couple_hbm, couple_ref),
        ))
    ]
    for copy in local_copies:
        copy.start()

    barrier = pltpu.get_barrier_semaphore()

    def greet(device):
        pl.semaphore_signal(barrier, inc=1, device_id=device, device_id_type=MESH)

    each(1, SEQ, lambda n: greet((dap, seq_peer(n))))

    def greet_left(n):
        px, pzh = left_peer(n)
        greet((dap_of(px, pzh, y), seq))

    each(1, LEFTS, greet_left)
    each(1, Y, lambda n: greet((dap_of(x, zh, y_peer(n)), seq)))

    def greet_tile(n):
        greet((dap_of(seq, lax.rem(zh + lax.div(n, SEQ), ZH), y), lax.rem(seq + lax.rem(n, SEQ), SEQ)))

    each(1, ZH * SEQ, greet_tile)
    pl.when(x != seq)(lambda: greet_tile(0))

    rows = lax.broadcasted_iota(jnp.int32, (SEQS, SEQS), 0)
    cols = lax.broadcasted_iota(jnp.int32, (SEQS, SEQS), 1)
    block = SEQS // SEQ
    by_residue = jnp.where(cols == rows % block * SEQ + rows // block, 1.0, 0.0).astype(BF16)
    for copy in local_copies:
        copy.wait()
    stack_send[...] = dot(by_residue, stack_ref[...].reshape(SEQS, FEATURES)).astype(BF16).reshape(
        SEQ, block, FEATURES)
    ident = eye(FEATURES)
    for n, ref in enumerate((asking_ref, lookup_ref, content_ref, sigmoid_ref)):
        wt[n * FEATURES:(n + 1) * FEATURES, :] = dot_t(ident, ref[...]).astype(BF16)
    wt_final[...] = dot_t(ident, final_ref[...]).astype(BF16)
    wt_pair[:PROJECTED_DIM, :] = former_ref[...]
    wt_pair[PROJECTED_DIM:, :] = latter_ref[...]
    couple[...] = couple_ref[...].astype(BF16)
    flags = homolog_ref[...].astype(F32)
    diagonal = (ident.astype(F32) * flags).astype(BF16)
    key_mask[...] = dot(diagonal, jnp.ones((SEQS, SEQS), BF16))
    count = jnp.sum(flags, axis=1, keepdims=True)
    residues = amino_ref.shape[1]
    shape = (ROWS_PICKED, residues)
    rows = lax.broadcasted_iota(jnp.int32, shape, 0)
    cols = lax.broadcasted_iota(jnp.int32, shape, 1)
    wanted = jnp.where(
        rows < RIGHTS, rows + dap_of(x, zh, 0) * SEQ,
        jnp.where(rows < RIGHTS + LEFTS, (rows - RIGHTS) * RIGHTS + y * SEQ + seq, dap * SEQ + seq),
    )
    picked = jnp.where(cols == wanted, 1.0, 0.0).astype(BF16)
    amino_wide = jnp.broadcast_to(amino_ref[...].astype(F32), (PAIR, residues)).astype(BF16)
    amino_rows[...] = dot_t(picked, amino_wide)

    greeted = SEQ - 1 + LEFTS - 1 + Y - 1 + ZH * SEQ
    pl.when(x != seq)(lambda: pl.semaphore_wait(barrier, greeted))
    pl.when(x == seq)(lambda: pl.semaphore_wait(barrier, greeted - 1))

    def stack_copy(n, slot):
        q = seq_peer(n)
        return copy_to(stack_send.at[q], stack_all.at[slot], stack_ss.at[n], stack_rs.at[slot], (dap, q))

    each(1, SEQ, lambda n: stack_copy(n, seq).start())
    stack_all[seq] = stack_send[seq]
    each(1, SEQ, lambda n: stack_copy(n, seq_peer(n)).wait_recv())

    incoming = dot_t(ident, stack_all[...].reshape(SEQS, FEATURES))
    normed = rescale_rows(incoming).astype(BF16)
    query = (dot(wt[0:256, :], normed) * PER_HEAD_DIM ** (-0.5)).astype(BF16)
    key_t = dot(wt[256:512, :], normed).astype(BF16)
    value = dot(wt[512:768, :], normed).astype(BF16)
    gate = jax.nn.sigmoid(dot(wt[768:1024, :], normed))
    key = dot_t(ident, key_t).astype(BF16)
    here = key_mask[...] > 0.5
    gated = []
    for h in range(HEADS):
        lo = h * PER_HEAD_DIM
        group = lo // 128 * 128
        before, after = lo - group, 128 - PER_HEAD_DIM - (lo - group)
        parts = [query[lo:lo + PER_HEAD_DIM]]
        if before:
            parts.insert(0, jnp.zeros((before, SEQS), BF16))
        if after:
            parts.append(jnp.zeros((after, SEQS), BF16))
        scores = dot(key[:, group:group + 128], jnp.concatenate(parts, axis=0))
        scores = jnp.where(here, scores, -1000000000.0)
        weights = jnp.exp(scores - jnp.max(scores, axis=0, keepdims=True))
        total = jnp.sum(weights, axis=0, keepdims=True)
        mixed = dot(value[lo:lo + PER_HEAD_DIM], weights.astype(BF16))
        gated.append((gate[lo:lo + PER_HEAD_DIM] * (mixed / total)).astype(BF16))
    gated = jnp.concatenate(gated, axis=0)
    attended = (incoming + dot(wt_final[...], gated)).astype(BF16)

    amino_here = amino_rows[RIGHTS + LEFTS:RIGHTS + LEFTS + 1, :]
    normed2 = rescale_rows(attended.astype(F32)).astype(BF16)
    sides = (dot(wt_pair[...], normed2) * (flags * jnp.concatenate([amino_here, amino_here], axis=1))).astype(BF16)

    def right_slot(core, py, pl_):
        return core * (Y * 2) + py * 2 + pl_

    def right_copy(pl_, py, send_sem, device):
        slot = right_slot(c, py, pl_)
        return copy_to(right_all.at[slot], right_all.at[slot], send_sem, right_rs.at[slot], device)

    def right_arrived(slot):
        copy_to(right_all.at[slot], right_all.at[slot], right_ls.at[0], right_rs.at[slot], (dap, seq)).wait_recv()

    other_l = (dap, (1 - l) * 2 + c)
    other_core = (dap, l * 2 + 1 - c)
    right_all[right_slot(c, y, l)] = sides[PROJECTED_DIM:]
    right_copy(l, y, right_ls.at[0], other_l).start()

    def to_y(pl_, sems, n):
        return right_copy(pl_, y, sems.at[n], (dap_of(x, zh, y_peer(n)), seq))

    each(1, Y, lambda n: to_y(l, right_ys, n).start())

    def to_core(py, pl_):
        return right_copy(pl_, py, right_cs.at[py * 2 + pl_], other_core)

    to_core(y, l).start()

    left_all[x * ZH + zh] = sides[:PROJECTED_DIM]

    def left_copy(n, slot):
        px, pzh = left_peer(n)
        return copy_to(
            left_all.at[slot], left_all.at[slot], left_ss.at[n], left_rs.at[slot],
            (dap_of(px, pzh, y), seq),
        )

    each(1, LEFTS, lambda n: left_copy(n, x * ZH + zh).start())

    right_arrived(right_slot(c, y, 1 - l))
    each(1, Y, lambda n: to_y(1 - l, right_fs, n).start())
    to_core(y, 1 - l).start()

    att_send[...] = dot_t(ident, attended).astype(BF16).reshape(SEQ, SEQS // SEQ, FEATURES)

    def att_copy(n, slot):
        q = seq_peer(n)
        return copy_to(att_send.at[q], att_ref.at[slot], att_ss.at[n], att_rs.at[slot], (dap, q))

    each(1, SEQ, lambda n: att_copy(n, seq).start())
    att_ref[seq] = att_send[seq]

    def pass_on(pl_, n):
        py = y_peer(n)
        right_arrived(right_slot(c, py, pl_))
        to_core(py, pl_).start()

    each(1, Y, lambda n: pass_on(l, n))
    each(1, Y, lambda n: pass_on(1 - l, n))

    def left_arrived(n):
        px, pzh = left_peer(n)
        left_copy(n, px * ZH + pzh).wait_recv()

    each(1, LEFTS, left_arrived)

    lefts = left_all[...].reshape(LEFTS * PROJECTED_DIM, SEQS).astype(F32)
    left_wide[0] = lefts[:, :128]
    left_wide[1] = lefts[:, 128:]
    each(0, Y * 2, lambda n: right_arrived(right_slot(1 - c, lax.div(n, 2), lax.rem(n, 2))))

    groups = PROJECTED_DIM // 4
    for k in range(4):
        left_k = jnp.concatenate(
            [jnp.concatenate(
                [left_wide[half, pl.ds(4 * g + k, LEFTS, stride=PROJECTED_DIM), :]
                 for half in range(2)], axis=1)
             for g in range(groups)], axis=0).astype(BF16)
        blocks = []
        for py in range(Y):
            for m in range(4):
                j = (m - k) % 4
                blocks.append(right_all[(j % 2) * (Y * 2) + py * 2 + j // 2])
        outer[k] = dot_t(left_k, jnp.concatenate(blocks, axis=0))

    lane_block = lax.broadcasted_iota(jnp.int32, (groups * LEFTS, 128), 1) // PROJECTED_DIM
    for a in range(4):
        flat = []
        for py in range(Y):
            cols = slice(py * 128, (py + 1) * 128)
            chosen = outer[(3 - a) % 4, :, cols]
            for m in range(3):
                chosen = jnp.where(lane_block == m, outer[(m - a) % 4, :, cols], chosen)
            chosen = chosen.astype(BF16)
            flat.append(jnp.concatenate(
                [chosen[g * LEFTS:(g + 1) * LEFTS] for g in range(groups)], axis=1))
        rows_a = jnp.concatenate(
            [couple[(4 * g + (m - a) % 4) * PROJECTED_DIM:(4 * g + (m - a) % 4 + 1) * PROJECTED_DIM, :]
             for g in range(groups) for m in range(4)], axis=0)
        result = dot(jnp.concatenate(flat, axis=0), rows_a)
        for py in range(Y):
            at = (py * 4 + a) * LEFTS
            projected[at:at + LEFTS, :] = result[py * LEFTS:(py + 1) * LEFTS]

    norm_cols = amino_rows[:RIGHTS, :] * count
    for i in range(LEFTS):
        norm = jnp.maximum(norm_cols * amino_rows[RIGHTS + i:RIGHTS + i + 1, :], 1.0)
        tiles[i] = (projected[pl.ds(i, RIGHTS, stride=LEFTS), :] / norm).astype(BF16)

    def tile_copy(n):
        px, pzh = left_peer(n)
        return copy_to(
            tiles.at[px * ZH + pzh],
            pair_ref.at[seq, pl.ds(pl.multiple_of(zh * RIGHTS, RIGHTS), RIGHTS)],
            tile_ss.at[n], tile_rs.at[zh * SEQ + seq],
            (dap_of(px, pzh, y), x),
        )

    def own_tile():
        return pltpu.make_async_copy(
            tiles.at[x * ZH + zh],
            pair_ref.at[seq, pl.ds(pl.multiple_of(zh * RIGHTS, RIGHTS), RIGHTS)],
            tile_rs.at[zh * SEQ + seq],
        )

    pl.when(x != seq)(lambda: tile_copy(0).start())
    pl.when(x == seq)(lambda: own_tile().start())
    each(1, LEFTS, lambda n: tile_copy(n).start())

    def tile_arrived(n):
        pzh, pseq = lax.div(n, SEQ), lax.rem(n, SEQ)
        pltpu.make_async_copy(
            tiles.at[0], pair_ref.at[pseq, pl.ds(pl.multiple_of(pzh * RIGHTS, RIGHTS), RIGHTS)],
            tile_rs.at[n],
        ).wait()

    each(0, ZH * SEQ, tile_arrived)
    each(1, SEQ, lambda n: att_copy(n, seq_peer(n)).wait_recv())

    each(1, SEQ, lambda n: stack_copy(n, seq).wait_send())
    each(1, SEQ, lambda n: att_copy(n, seq).wait_send())
    each(1, LEFTS, lambda n: left_copy(n, x * ZH + zh).wait_send())
    right_copy(l, y, right_ls.at[0], other_l).wait_send()
    each(1, Y, lambda n: to_y(l, right_ys, n).wait_send())
    each(1, Y, lambda n: to_y(1 - l, right_fs, n).wait_send())
    each(0, Y * 2, lambda n: to_core(lax.div(n, 2), lax.rem(n, 2)).wait_send())
    pl.when(x != seq)(lambda: tile_copy(0).wait_send())
    each(1, LEFTS, lambda n: tile_copy(n).wait_send())


def on_device(
    homolog_stack,
    homolog_existing_flags,
    amino_existing_flags,
    asking_weights,
    lookup_weights,
    content_weights,
    sigmoid_weights,
    final_projection,
    former_weights,
    latter_weights,
    couple_projection,
):
    block = SEQS // SEQ
    vmem = pl.BlockSpec(memory_space=pltpu.VMEM)
    hbm = pl.BlockSpec(memory_space=pltpu.HBM)
    dma = pltpu.SemaphoreType.DMA
    operands = (
        homolog_stack,
        homolog_existing_flags[None, :],
        amino_existing_flags[None, :],
        asking_weights, lookup_weights, content_weights, sigmoid_weights, final_projection,
        former_weights.T, latter_weights.T, couple_projection,
    )
    attended, pair = pl.pallas_call(
        kernel,
        out_shape=(
            pltpu.VMEM((SEQ, block, FEATURES), BF16),
            pltpu.VMEM((SEQ, ZH * RIGHTS, PAIR), BF16),
        ),
        in_specs=[hbm] * len(operands),
        out_specs=(vmem, vmem),
        scratch_shapes=[pltpu.VMEM(a.shape, a.dtype) for a in operands] + [
            dma((len(operands),)),
            pltpu.VMEM((SEQ, block, FEATURES), BF16),
            pltpu.VMEM((SEQ, block, FEATURES), BF16),
            pltpu.VMEM((SEQ, block, FEATURES), BF16),
            pltpu.VMEM((LEFTS, PROJECTED_DIM, SEQS), BF16),
            pltpu.VMEM((RIGHTS, PROJECTED_DIM, SEQS), BF16),
            pltpu.VMEM((4 * FEATURES, FEATURES), BF16),
            pltpu.VMEM((FEATURES, FEATURES), BF16),
            pltpu.VMEM((2 * PROJECTED_DIM, FEATURES), BF16),
            pltpu.VMEM((PROJECTED_DIM * PROJECTED_DIM, PAIR), BF16),
            pltpu.VMEM((SEQS, SEQS), F32),
            pltpu.VMEM((2, LEFTS * PROJECTED_DIM, SEQS // 2), F32),
            pltpu.VMEM((4, PROJECTED_DIM // 4 * LEFTS, RIGHTS * PROJECTED_DIM), F32),
            pltpu.VMEM((RIGHTS * LEFTS, PAIR), F32),
            pltpu.VMEM((LEFTS, RIGHTS, PAIR), BF16),
            pltpu.VMEM((ROWS_PICKED, PAIR), F32),
            dma((SEQ,)), dma((SEQ,)), dma((SEQ,)), dma((SEQ,)),
            dma((LEFTS,)), dma((LEFTS,)),
            dma((1,)), dma((Y,)), dma((Y,)), dma((Y * 2,)), dma((RIGHTS,)),
            dma((LEFTS,)), dma((ZH * SEQ,)),
        ],
        compiler_params=pltpu.CompilerParams(
            collective_id=0, has_side_effects=True, vmem_limit_bytes=60 * 2**20
        ),
        name="column_attention_outer_product",
    )(*operands)
    return attended.transpose(1, 0, 2), pair


def solution(mesh):
    in_specs = (P("seq", "dap", None), P(), P(), P(), P(), P(), P(), P(), P(), P(), P())
    out_specs = (P("seq", "dap", None), P("dap", "seq", None))
    return jax.shard_map(
        on_device, mesh=mesh, in_specs=in_specs, out_specs=out_specs, check_vma=False
    )
```

```python
import functools

import jax
import jax.numpy as jnp
from jax import lax
from jax.experimental import pallas as pl
from jax.experimental.pallas import tpu as pltpu
from jax.sharding import PartitionSpec as P

HEADS = 8
PER_HEAD_DIM = 32
PROJECTED_DIM = 32
PAIR = 128
FEATURES = 256
SEQS = 256
X, ZH, Y, SEQ = 4, 4, 8, 4
ROWS_PICKED = 64
LEFTS = X * ZH
RIGHTS = Y * SEQ
MESH = pl.DeviceIdType.MESH
F32 = jnp.float32
BF16 = jnp.bfloat16


def dot(a, b):
    return lax.dot_general(a, b, (((1,), (0,)), ((), ())), preferred_element_type=F32)


def dot_t(a, b):
    return lax.dot_general(a, b, (((1,), (1,)), ((), ())), preferred_element_type=F32)


def eye(size):
    rows = lax.broadcasted_iota(jnp.int32, (size, size), 0)
    cols = lax.broadcasted_iota(jnp.int32, (size, size), 1)
    return jnp.where(rows == cols, 1.0, 0.0).astype(BF16)


def rescale_rows(values):
    mean = jnp.mean(values, axis=0, keepdims=True)
    centred = values - mean
    variance = jnp.mean(centred * centred, axis=0, keepdims=True)
    return centred * lax.rsqrt(variance + 1e-05)


def kernel(
    stack_hbm, homolog_hbm, amino_hbm, asking_hbm, lookup_hbm, content_hbm, sigmoid_hbm, final_hbm,
    former_hbm, latter_hbm, couple_hbm,
    att_ref, pair_ref,
    stack_ref, homolog_ref, amino_ref, asking_ref, lookup_ref, content_ref, sigmoid_ref, final_ref,
    former_ref, latter_ref, couple_ref, local_sems,
    stack_send, stack_all, att_send, left_all, right_all, wt, wt_final, wt_pair, couple, key_mask,
    left_wide, outer, projected, tiles, amino_rows,
    here_sems, stack_ss, stack_rs, att_ss, att_rs, left_ss, left_rs,
    right_ls, right_ys, right_fs, right_cs, right_rs, tile_ss, tile_rs,
):
    dap = lax.axis_index("dap")
    seq = lax.axis_index("seq")
    x, zh, y = lax.div(dap, ZH * Y), lax.rem(lax.div(dap, Y), ZH), lax.rem(dap, Y)
    l, c = lax.div(seq, 2), lax.rem(seq, 2)

    def dap_of(px, pzh, py):
        return (px * ZH + pzh) * Y + py

    def seq_peer(n):
        return lax.rem(seq + n, SEQ)

    def left_peer(n):
        return lax.rem(x + lax.div(n, ZH), X), lax.rem(zh + lax.rem(n, ZH), ZH)

    def y_peer(n):
        odd = lax.rem(n, 2)
        half = lax.div(n, 2)
        step = odd * (half + 1) + (1 - odd) * (Y - half)
        return lax.rem(y + step, Y)

    def copy_to(src, dst, send_sem, recv_sem, device):
        return pltpu.make_async_remote_copy(
            src_ref=src, dst_ref=dst, send_sem=send_sem, recv_sem=recv_sem,
            device_id=device, device_id_type=MESH,
        )

    def each(lo, hi, body):
        def step(n, carry):
            body(n)
            return carry
        lax.fori_loop(lo, hi, step, 0)

    local_copies = [
        pltpu.make_async_copy(src, dst, local_sems.at[n])
        for n, (src, dst) in enumerate((
            (stack_hbm, stack_ref), (asking_hbm, asking_ref), (lookup_hbm, lookup_ref),
            (content_hbm, content_ref), (sigmoid_hbm, sigmoid_ref), (final_hbm, final_ref),
            (former_hbm, former_ref), (latter_hbm, latter_ref), (homolog_hbm, homolog_ref),
            (amino_hbm, amino_ref), (couple_hbm, couple_ref),
        ))
    ]
    for copy in local_copies:
        copy.start()

    barrier = pltpu.get_barrier_semaphore()

    def greet(device):
        pl.semaphore_signal(barrier, inc=1, device_id=device, device_id_type=MESH)

    def along_x(n):
        return lax.rem(x + n, X)

    each(1, SEQ, lambda n: greet((dap, seq_peer(n))))
    each(1, X, lambda n: greet((dap_of(along_x(n), zh, y), seq)))
    each(1, Y, lambda n: greet((dap_of(x, zh, y_peer(n)), seq)))
    above = (ZH - 1 - zh) * X
    below = zh * X

    def peer_above(n):
        return along_x(lax.rem(n, X)), zh + 1 + lax.div(n, X)

    def peer_below(n):
        return along_x(lax.rem(n, X)), zh - 1 - lax.div(n, X)

    def greet_above(n):
        px, pzh = peer_above(n)
        greet((dap_of(px, pzh, y), seq))

    each(0, above, greet_above)

    rows = lax.broadcasted_iota(jnp.int32, (SEQS, SEQS), 0)
    cols = lax.broadcasted_iota(jnp.int32, (SEQS, SEQS), 1)
    block = SEQS // SEQ
    by_residue = jnp.where(cols == rows % block * SEQ + rows // block, 1.0, 0.0).astype(BF16)
    local_copies[0].wait()
    stack_send[...] = dot(by_residue, stack_ref[...].reshape(SEQS, FEATURES)).astype(BF16).reshape(
        SEQ, block, FEATURES)

    pl.semaphore_wait(barrier, SEQ - 1 + X - 1 + Y - 1 + below)

    def answer(n):
        px, pzh = peer_below(n)
        pl.semaphore_signal(
            here_sems.at[x * ZH + zh], inc=1, device_id=(dap_of(px, pzh, y), seq), device_id_type=MESH
        )

    each(0, below, answer)

    def stack_copy(n, slot):
        q = seq_peer(n)
        return copy_to(stack_send.at[q], stack_all.at[slot], stack_ss.at[n], stack_rs.at[slot], (dap, q))

    each(1, SEQ, lambda n: stack_copy(n, seq).start())
    stack_all[seq] = stack_send[seq]

    for copy in local_copies[1:]:
        copy.wait()
    ident = eye(FEATURES)
    for n, ref in enumerate((asking_ref, lookup_ref, content_ref, sigmoid_ref)):
        wt[n * FEATURES:(n + 1) * FEATURES, :] = dot_t(ident, ref[...]).astype(BF16)
    wt_final[...] = dot_t(ident, final_ref[...]).astype(BF16)
    wt_pair[:PROJECTED_DIM, :] = former_ref[...]
    wt_pair[PROJECTED_DIM:, :] = latter_ref[...]
    couple[...] = couple_ref[...].astype(BF16)
    flags = homolog_ref[...].astype(F32)
    diagonal = (ident.astype(F32) * flags).astype(BF16)
    key_mask[...] = dot(diagonal, jnp.ones((SEQS, SEQS), BF16))
    count = jnp.sum(flags, axis=1, keepdims=True)
    residues = amino_ref.shape[1]
    shape = (ROWS_PICKED, residues)
    rows = lax.broadcasted_iota(jnp.int32, shape, 0)
    cols = lax.broadcasted_iota(jnp.int32, shape, 1)
    wanted = jnp.where(
        rows < RIGHTS, rows + dap_of(x, zh, 0) * SEQ,
        jnp.where(rows < RIGHTS + LEFTS, (rows - RIGHTS) * RIGHTS + y * SEQ + seq, dap * SEQ + seq),
    )
    picked = jnp.where(cols == wanted, 1.0, 0.0).astype(BF16)
    amino_wide = jnp.broadcast_to(amino_ref[...].astype(F32), (PAIR, residues)).astype(BF16)
    amino_rows[...] = dot_t(picked, amino_wide)

    each(1, SEQ, lambda n: stack_copy(n, seq_peer(n)).wait_recv())

    incoming = dot_t(ident, stack_all[...].reshape(SEQS, FEATURES))
    normed = rescale_rows(incoming).astype(BF16)
    query = (dot(wt[0:256, :], normed) * PER_HEAD_DIM ** (-0.5)).astype(BF16)
    key_t = dot(wt[256:512, :], normed).astype(BF16)
    value = dot(wt[512:768, :], normed).astype(BF16)
    gate = jax.nn.sigmoid(dot(wt[768:1024, :], normed))
    key = dot_t(ident, key_t).astype(BF16)
    here = key_mask[...] > 0.5
    gated = []
    for h in range(HEADS):
        lo = h * PER_HEAD_DIM
        group = lo // 128 * 128
        before, after = lo - group, 128 - PER_HEAD_DIM - (lo - group)
        parts = [query[lo:lo + PER_HEAD_DIM]]
        if before:
            parts.insert(0, jnp.zeros((before, SEQS), BF16))
        if after:
            parts.append(jnp.zeros((after, SEQS), BF16))
        scores = dot(key[:, group:group + 128], jnp.concatenate(parts, axis=0))
        scores = jnp.where(here, scores, -1000000000.0)
        weights = jnp.exp(scores - jnp.max(scores, axis=0, keepdims=True))
        total = jnp.sum(weights, axis=0, keepdims=True)
        mixed = dot(value[lo:lo + PER_HEAD_DIM], weights.astype(BF16))
        gated.append((gate[lo:lo + PER_HEAD_DIM] * (mixed / total)).astype(BF16))
    gated = jnp.concatenate(gated, axis=0)
    attended = (incoming + dot(wt_final[...], gated)).astype(BF16)

    amino_here = amino_rows[RIGHTS + LEFTS:RIGHTS + LEFTS + 1, :]
    normed2 = rescale_rows(attended.astype(F32)).astype(BF16)
    sides = (dot(wt_pair[...], normed2) * (flags * jnp.concatenate([amino_here, amino_here], axis=1))).astype(BF16)

    def right_slot(core, py, pl_):
        return core * (Y * 2) + py * 2 + pl_

    def right_copy(pl_, py, send_sem, device):
        slot = right_slot(c, py, pl_)
        return copy_to(right_all.at[slot], right_all.at[slot], send_sem, right_rs.at[slot], device)

    def right_arrived(slot):
        copy_to(right_all.at[slot], right_all.at[slot], right_ls.at[0], right_rs.at[slot], (dap, seq)).wait_recv()

    other_l = (dap, (1 - l) * 2 + c)
    other_core = (dap, l * 2 + 1 - c)
    right_all[right_slot(c, y, l)] = sides[PROJECTED_DIM:]
    right_copy(l, y, right_ls.at[0], other_l).start()

    def to_y(pl_, sems, n):
        return right_copy(pl_, y, sems.at[n], (dap_of(x, zh, y_peer(n)), seq))

    each(1, Y, lambda n: to_y(l, right_ys, n).start())

    def to_core(py, pl_):
        return right_copy(pl_, py, right_cs.at[py * 2 + pl_], other_core)

    to_core(y, l).start()

    left_all[x * ZH + zh] = sides[:PROJECTED_DIM]

    def left_copy(px, pzh, slot):
        there = px * ZH + pzh
        return copy_to(
            left_all.at[slot], left_all.at[slot], left_ss.at[there], left_rs.at[slot],
            (dap_of(px, pzh, y), seq),
        )

    def left_send(px, pzh):
        left_copy(px, pzh, x * ZH + zh).start()

    each(0, below, lambda n: left_send(*peer_below(n)))
    each(1, X, lambda n: left_send(along_x(n), zh))

    right_arrived(right_slot(c, y, 1 - l))
    each(1, Y, lambda n: to_y(1 - l, right_fs, n).start())
    to_core(y, 1 - l).start()

    def left_send_above(n):
        px, pzh = peer_above(n)
        pl.semaphore_wait(here_sems.at[px * ZH + pzh], 1)
        left_send(px, pzh)

    each(0, above, left_send_above)

    att_send[...] = dot_t(ident, attended).astype(BF16).reshape(SEQ, SEQS // SEQ, FEATURES)

    def att_copy(n, slot):
        q = seq_peer(n)
        return copy_to(att_send.at[q], att_ref.at[slot], att_ss.at[n], att_rs.at[slot], (dap, q))

    each(1, SEQ, lambda n: att_copy(n, seq).start())
    att_ref[seq] = att_send[seq]

    def pass_on(pl_, n):
        py = y_peer(n)
        right_arrived(right_slot(c, py, pl_))
        to_core(py, pl_).start()

    each(1, Y, lambda n: pass_on(l, n))
    each(1, Y, lambda n: pass_on(1 - l, n))

    def left_arrived(n):
        px, pzh = left_peer(n)
        left_copy(px, pzh, px * ZH + pzh).wait_recv()

    each(1, LEFTS, left_arrived)

    lefts = left_all[...].reshape(LEFTS * PROJECTED_DIM, SEQS).astype(F32)
    left_wide[0] = lefts[:, :128]
    left_wide[1] = lefts[:, 128:]
    each(0, Y * 2, lambda n: right_arrived(right_slot(1 - c, lax.div(n, 2), lax.rem(n, 2))))

    groups = PROJECTED_DIM // 4
    for k in range(4):
        left_k = jnp.concatenate(
            [jnp.concatenate(
                [left_wide[half, pl.ds(4 * g + k, LEFTS, stride=PROJECTED_DIM), :]
                 for half in range(2)], axis=1)
             for g in range(groups)], axis=0).astype(BF16)
        blocks = []
        for py in range(Y):
            for m in range(4):
                j = (m - k) % 4
                blocks.append(right_all[(j % 2) * (Y * 2) + py * 2 + j // 2])
        outer[k] = dot_t(left_k, jnp.concatenate(blocks, axis=0))

    lane_block = lax.broadcasted_iota(jnp.int32, (groups * LEFTS, 128), 1) // PROJECTED_DIM
    for a in range(4):
        flat = []
        for py in range(Y):
            cols = slice(py * 128, (py + 1) * 128)
            chosen = outer[(3 - a) % 4, :, cols]
            for m in range(3):
                chosen = jnp.where(lane_block == m, outer[(m - a) % 4, :, cols], chosen)
            chosen = chosen.astype(BF16)
            flat.append(jnp.concatenate(
                [chosen[g * LEFTS:(g + 1) * LEFTS] for g in range(groups)], axis=1))
        rows_a = jnp.concatenate(
            [couple[(4 * g + (m - a) % 4) * PROJECTED_DIM:(4 * g + (m - a) % 4 + 1) * PROJECTED_DIM, :]
             for g in range(groups) for m in range(4)], axis=0)
        result = dot(jnp.concatenate(flat, axis=0), rows_a)
        for py in range(Y):
            at = (py * 4 + a) * LEFTS
            projected[at:at + LEFTS, :] = result[py * LEFTS:(py + 1) * LEFTS]

    norm_cols = amino_rows[:RIGHTS, :] * count
    for i in range(LEFTS):
        norm = jnp.maximum(norm_cols * amino_rows[RIGHTS + i:RIGHTS + i + 1, :], 1.0)
        tiles[i] = (projected[pl.ds(i, RIGHTS, stride=LEFTS), :] / norm).astype(BF16)

    def tile_copy(n):
        px, pzh = left_peer(n)
        return copy_to(
            tiles.at[px * ZH + pzh],
            pair_ref.at[seq, pl.ds(pl.multiple_of(zh * RIGHTS, RIGHTS), RIGHTS)],
            tile_ss.at[n], tile_rs.at[zh * SEQ + seq],
            (dap_of(px, pzh, y), x),
        )

    def own_tile():
        return pltpu.make_async_copy(
            tiles.at[x * ZH + zh],
            pair_ref.at[seq, pl.ds(pl.multiple_of(zh * RIGHTS, RIGHTS), RIGHTS)],
            tile_rs.at[zh * SEQ + seq],
        )

    pl.when(x != seq)(lambda: tile_copy(0).start())
    pl.when(x == seq)(lambda: own_tile().start())
    each(1, LEFTS, lambda n: tile_copy(n).start())

    def tile_arrived(n):
        pzh, pseq = lax.div(n, SEQ), lax.rem(n, SEQ)
        pltpu.make_async_copy(
            tiles.at[0], pair_ref.at[pseq, pl.ds(pl.multiple_of(pzh * RIGHTS, RIGHTS), RIGHTS)],
            tile_rs.at[n],
        ).wait()

    each(0, ZH * SEQ, tile_arrived)
    each(1, SEQ, lambda n: att_copy(n, seq_peer(n)).wait_recv())

    each(1, SEQ, lambda n: stack_copy(n, seq).wait_send())
    each(1, SEQ, lambda n: att_copy(n, seq).wait_send())

    def left_gone(n):
        px, pzh = left_peer(n)
        left_copy(px, pzh, x * ZH + zh).wait_send()

    each(1, LEFTS, left_gone)
    right_copy(l, y, right_ls.at[0], other_l).wait_send()
    each(1, Y, lambda n: to_y(l, right_ys, n).wait_send())
    each(1, Y, lambda n: to_y(1 - l, right_fs, n).wait_send())
    each(0, Y * 2, lambda n: to_core(lax.div(n, 2), lax.rem(n, 2)).wait_send())
    pl.when(x != seq)(lambda: tile_copy(0).wait_send())
    each(1, LEFTS, lambda n: tile_copy(n).wait_send())


def on_device(
    homolog_stack,
    homolog_existing_flags,
    amino_existing_flags,
    asking_weights,
    lookup_weights,
    content_weights,
    sigmoid_weights,
    final_projection,
    former_weights,
    latter_weights,
    couple_projection,
):
    block = SEQS // SEQ
    vmem = pl.BlockSpec(memory_space=pltpu.VMEM)
    hbm = pl.BlockSpec(memory_space=pltpu.HBM)
    dma = pltpu.SemaphoreType.DMA
    operands = (
        homolog_stack,
        homolog_existing_flags[None, :],
        amino_existing_flags[None, :],
        asking_weights, lookup_weights, content_weights, sigmoid_weights, final_projection,
        former_weights.T, latter_weights.T, couple_projection,
    )
    attended, pair = pl.pallas_call(
        kernel,
        out_shape=(
            pltpu.VMEM((SEQ, block, FEATURES), BF16),
            pltpu.VMEM((SEQ, ZH * RIGHTS, PAIR), BF16),
        ),
        in_specs=[hbm] * len(operands),
        out_specs=(vmem, vmem),
        scratch_shapes=[pltpu.VMEM(a.shape, a.dtype) for a in operands] + [
            dma((len(operands),)),
            pltpu.VMEM((SEQ, block, FEATURES), BF16),
            pltpu.VMEM((SEQ, block, FEATURES), BF16),
            pltpu.VMEM((SEQ, block, FEATURES), BF16),
            pltpu.VMEM((LEFTS, PROJECTED_DIM, SEQS), BF16),
            pltpu.VMEM((RIGHTS, PROJECTED_DIM, SEQS), BF16),
            pltpu.VMEM((4 * FEATURES, FEATURES), BF16),
            pltpu.VMEM((FEATURES, FEATURES), BF16),
            pltpu.VMEM((2 * PROJECTED_DIM, FEATURES), BF16),
            pltpu.VMEM((PROJECTED_DIM * PROJECTED_DIM, PAIR), BF16),
            pltpu.VMEM((SEQS, SEQS), F32),
            pltpu.VMEM((2, LEFTS * PROJECTED_DIM, SEQS // 2), F32),
            pltpu.VMEM((4, PROJECTED_DIM // 4 * LEFTS, RIGHTS * PROJECTED_DIM), F32),
            pltpu.VMEM((RIGHTS * LEFTS, PAIR), F32),
            pltpu.VMEM((LEFTS, RIGHTS, PAIR), BF16),
            pltpu.VMEM((ROWS_PICKED, PAIR), F32),
            pltpu.SemaphoreType.REGULAR((LEFTS,)),
            dma((SEQ,)), dma((SEQ,)), dma((SEQ,)), dma((SEQ,)),
            dma((LEFTS,)), dma((LEFTS,)),
            dma((1,)), dma((Y,)), dma((Y,)), dma((Y * 2,)), dma((RIGHTS,)),
            dma((LEFTS,)), dma((ZH * SEQ,)),
        ],
        compiler_params=pltpu.CompilerParams(
            collective_id=0, has_side_effects=True, vmem_limit_bytes=60 * 2**20
        ),
        name="column_attention_outer_product",
    )(*operands)
    return attended.transpose(1, 0, 2), pair


def solution(mesh):
    in_specs = (P("seq", "dap", None), P(), P(), P(), P(), P(), P(), P(), P(), P(), P())
    out_specs = (P("seq", "dap", None), P("dap", "seq", None))
    return jax.shard_map(
        on_device, mesh=mesh, in_specs=in_specs, out_specs=out_specs, check_vma=False
    )
```

```python
import functools

import jax
import jax.numpy as jnp
from jax import lax
from jax.experimental import pallas as pl
from jax.experimental.pallas import tpu as pltpu
from jax.sharding import PartitionSpec as P

HEADS = 8
PER_HEAD_DIM = 32
PROJECTED_DIM = 32
PAIR = 128
FEATURES = 256
SEQS = 256
X, ZH, Y, SEQ = 4, 4, 8, 4
ROWS_PICKED = 64
LEFTS = X * ZH * 2
RIGHTS = Y * 2
PLANE = X * 2
TILES = X * ZH
MESH = pl.DeviceIdType.MESH
F32 = jnp.float32
BF16 = jnp.bfloat16


def dot(a, b):
    return lax.dot_general(a, b, (((1,), (0,)), ((), ())), preferred_element_type=F32)


def dot_t(a, b):
    return lax.dot_general(a, b, (((1,), (1,)), ((), ())), preferred_element_type=F32)


def eye(size):
    rows = lax.broadcasted_iota(jnp.int32, (size, size), 0)
    cols = lax.broadcasted_iota(jnp.int32, (size, size), 1)
    return jnp.where(rows == cols, 1.0, 0.0).astype(BF16)


def rescale_rows(values):
    mean = jnp.mean(values, axis=0, keepdims=True)
    centred = values - mean
    variance = jnp.mean(centred * centred, axis=0, keepdims=True)
    return centred * lax.rsqrt(variance + 1e-05)


def kernel(
    stack_hbm, homolog_hbm, amino_hbm, asking_hbm, lookup_hbm, content_hbm, sigmoid_hbm, final_hbm,
    former_hbm, latter_hbm, couple_hbm,
    att_ref, pair_ref,
    stack_ref, homolog_ref, amino_ref, asking_ref, lookup_ref, content_ref, sigmoid_ref, final_ref,
    former_ref, latter_ref, couple_ref, local_sems,
    stack_send, stack_all, att_send, left_all, right_all, wt, wt_final, wt_pair, couple, key_mask,
    left_wide, outer, projected, tiles, tiles_in, pair_wide, amino_rows,
    here_sems, stack_ss, stack_rs, att_ss, att_rs, left_ss, left_rs,
    right_ss, right_rs, tile_ss, tile_rs,
):
    dap = lax.axis_index("dap")
    seq = lax.axis_index("seq")
    x, zh, y = lax.div(dap, ZH * Y), lax.rem(lax.div(dap, Y), ZH), lax.rem(dap, Y)
    l, c = lax.div(seq, 2), lax.rem(seq, 2)

    def dap_of(px, pzh, py):
        return (px * ZH + pzh) * Y + py

    xs = [x] + [lax.rem(x + n, X) for n in range(1, X)]
    zs = [zh] + [lax.rem(zh + n, ZH) for n in range(1, ZH)]
    ys = [y] + [lax.rem(y + n, Y) for n in range(1, Y)]
    qs = [seq] + [lax.rem(seq + n, SEQ) for n in range(1, SEQ)]

    def copy_to(src, dst, send_sem, recv_sem, device):
        return pltpu.make_async_remote_copy(
            src_ref=src, dst_ref=dst, send_sem=send_sem, recv_sem=recv_sem,
            device_id=device, device_id_type=MESH,
        )

    def each(lo, hi, body):
        def step(n, carry):
            body(n)
            return carry
        lax.fori_loop(lo, hi, step, 0)

    local_copies = [
        pltpu.make_async_copy(src, dst, local_sems.at[n])
        for n, (src, dst) in enumerate((
            (stack_hbm, stack_ref), (asking_hbm, asking_ref), (lookup_hbm, lookup_ref),
            (content_hbm, content_ref), (sigmoid_hbm, sigmoid_ref), (final_hbm, final_ref),
            (former_hbm, former_ref), (latter_hbm, latter_ref), (homolog_hbm, homolog_ref),
            (amino_hbm, amino_ref), (couple_hbm, couple_ref),
        ))
    ]
    local_copies[0].start()

    barrier = pltpu.get_barrier_semaphore()

    def greet(device):
        pl.semaphore_signal(barrier, inc=1, device_id=device, device_id_type=MESH)

    for q in qs[1:]:
        greet((dap, q))
    for py in ys[1:]:
        greet((dap_of(x, zh, py), seq))
    for px in xs[1:]:
        greet((dap_of(px, zh, y), seq))
    each(zh + 1, ZH, lambda pzh: greet((dap_of(x, pzh, y), seq)))
    for copy in local_copies[1:]:
        copy.start()

    rows = lax.broadcasted_iota(jnp.int32, (SEQS, SEQS), 0)
    cols = lax.broadcasted_iota(jnp.int32, (SEQS, SEQS), 1)
    block = SEQS // SEQ
    by_residue = jnp.where(cols == rows % block * SEQ + rows // block, 1.0, 0.0).astype(BF16)
    local_copies[0].wait()
    stack_send[...] = dot(by_residue, stack_ref[...].reshape(SEQS, FEATURES)).astype(BF16).reshape(
        SEQ, block, FEATURES)

    pl.semaphore_wait(barrier, SEQ - 1 + X - 1 + Y - 1 + zh)

    def stack_copy(n, slot):
        return copy_to(
            stack_send.at[qs[n]], stack_all.at[slot], stack_ss.at[n], stack_rs.at[slot], (dap, qs[n]))

    for n in range(1, SEQ):
        stack_copy(n, seq).start()

    def answer(pzh):
        pl.semaphore_signal(
            here_sems.at[zh], inc=1, device_id=(dap_of(x, pzh, y), seq), device_id_type=MESH)

    each(0, zh, answer)
    stack_all[seq] = stack_send[seq]

    for copy in local_copies[1:]:
        copy.wait()
    ident = eye(FEATURES)
    for n, ref in enumerate((asking_ref, lookup_ref, content_ref, sigmoid_ref)):
        wt[n * FEATURES:(n + 1) * FEATURES, :] = dot_t(ident, ref[...]).astype(BF16)
    wt_final[...] = dot_t(ident, final_ref[...]).astype(BF16)
    wt_pair[:PROJECTED_DIM, :] = former_ref[...]
    wt_pair[PROJECTED_DIM:, :] = latter_ref[...]
    couple[...] = couple_ref[...].astype(BF16)
    flags = homolog_ref[...].astype(F32)
    diagonal = (ident.astype(F32) * flags).astype(BF16)
    key_mask[...] = dot(diagonal, jnp.ones((SEQS, SEQS), BF16))
    count = jnp.sum(flags, axis=1, keepdims=True)
    residues = amino_ref.shape[1]
    shape = (ROWS_PICKED, residues)
    rows = lax.broadcasted_iota(jnp.int32, shape, 0)
    cols = lax.broadcasted_iota(jnp.int32, shape, 1)
    wanted = jnp.where(
        rows < RIGHTS, dap_of(x, zh, 0) * SEQ + 2 * rows + c,
        jnp.where(
            rows < RIGHTS + LEFTS,
            dap_of((rows - RIGHTS) % X, (rows - RIGHTS) // PLANE, y) * SEQ + 2 * l
            + (rows - RIGHTS) // X % 2,
            dap * SEQ + seq,
        ),
    )
    picked = jnp.where(cols == wanted, 1.0, 0.0).astype(BF16)
    amino_wide = jnp.broadcast_to(amino_ref[...].astype(F32), (PAIR, residues)).astype(BF16)
    amino_rows[...] = dot_t(picked, amino_wide)

    for n in range(1, SEQ):
        stack_copy(n, qs[n]).wait_recv()

    incoming = dot_t(ident, stack_all[...].reshape(SEQS, FEATURES))
    normed = rescale_rows(incoming).astype(BF16)
    query = (dot(wt[0:256, :], normed) * PER_HEAD_DIM ** (-0.5)).astype(BF16)
    key_t = dot(wt[256:512, :], normed).astype(BF16)
    value = dot(wt[512:768, :], normed).astype(BF16)
    gate = jax.nn.sigmoid(dot(wt[768:1024, :], normed))
    key = dot_t(ident, key_t).astype(BF16)
    here = key_mask[...] > 0.5
    gated = []
    for h in range(HEADS):
        lo = h * PER_HEAD_DIM
        group = lo // 128 * 128
        before, after = lo - group, 128 - PER_HEAD_DIM - (lo - group)
        parts = [query[lo:lo + PER_HEAD_DIM]]
        if before:
            parts.insert(0, jnp.zeros((before, SEQS), BF16))
        if after:
            parts.append(jnp.zeros((after, SEQS), BF16))
        scores = dot(key[:, group:group + 128], jnp.concatenate(parts, axis=0))
        scores = jnp.where(here, scores, -1000000000.0)
        weights = jnp.exp(scores - jnp.max(scores, axis=0, keepdims=True))
        total = jnp.sum(weights, axis=0, keepdims=True)
        mixed = dot(value[lo:lo + PER_HEAD_DIM], weights.astype(BF16))
        gated.append((gate[lo:lo + PER_HEAD_DIM] * (mixed / total)).astype(BF16))
    gated = jnp.concatenate(gated, axis=0)
    attended = (incoming + dot(wt_final[...], gated)).astype(BF16)

    amino_here = amino_rows[RIGHTS + LEFTS:RIGHTS + LEFTS + 1, :]
    normed2 = rescale_rows(attended.astype(F32)).astype(BF16)
    sides = (dot(wt_pair[...], normed2) * (flags * jnp.concatenate([amino_here, amino_here], axis=1))).astype(BF16)

    def right_copy(slot, send_sem, device):
        ref = right_all.at[slot]
        return copy_to(ref, ref, send_sem, right_rs.at[slot], device)

    def right_arrived(slot):
        right_copy(slot, right_ss.at[0], (dap, qs[1])).wait_recv()

    other_l = (dap, (1 - l) * 2 + c)
    other_core = (dap, l * 2 + 1 - c)
    right_sent = []

    def send_right(slot, device):
        copy = right_copy(slot, right_ss.at[len(right_sent)], device)
        copy.start()
        right_sent.append(copy)

    own = y * 2 + l

    def left_slot(core, px, pzh):
        return pzh * PLANE + core * X + px

    def left_copy(px, pzh, n, device):
        slot = left_slot(c, px, pzh)
        return copy_to(left_all.at[slot], left_all.at[slot], left_ss.at[n], left_rs.at[slot], device)

    def along_z(pzh):
        return left_copy(x, zh, pzh, (dap_of(x, pzh, y), seq))

    def along_x(pzh, n):
        return left_copy(x, pzh, ZH + pzh * X + n, (dap_of(xs[n], zh, y), seq))

    def to_core(px, pzh):
        return left_copy(px, pzh, ZH + TILES + px * ZH + pzh, other_core)

    def spread(pzh):
        for n in (1, 3, 2):
            along_x(pzh, n).start()
        to_core(x, pzh).start()

    def left_arrived(px, pzh):
        left_copy(px, pzh, 0, (dap, qs[1])).wait_recv()

    def pass_left(pzh):
        left_arrived(x, pzh)
        spread(pzh)

    def take_left(pzh):
        for n in (1, 3, 2):
            left_arrived(xs[n], pzh)
            to_core(xs[n], pzh).start()

    left_all[left_slot(c, x, zh)] = sides[:PROJECTED_DIM]
    each(0, zh, lambda pzh: along_z(pzh).start())
    right_all[own] = sides[PROJECTED_DIM:]
    send_right(own, other_l)
    for n in (1, 7, 2, 6, 3, 5, 4):
        send_right(own, (dap_of(x, zh, ys[n]), seq))
    spread(zh)

    def send_above(pzh):
        pl.semaphore_wait(here_sems.at[pzh], 1)
        along_z(pzh).start()

    each(zh + 1, ZH, send_above)

    def pass_y(n):
        slot = ys[n] * 2 + l
        right_arrived(slot)
        send_right(slot, other_l)

    att_send[...] = dot_t(ident, attended).astype(BF16).reshape(SEQ, SEQS // SEQ, FEATURES)
    pass_y(1)
    pass_y(7)
    each(0, zh, pass_left)
    pass_y(2)
    pass_y(6)
    pass_y(3)
    pass_y(5)
    pass_y(4)
    each(0, zh + 1, take_left)

    def att_copy(n, slot):
        return copy_to(
            att_send.at[qs[n]], att_ref.at[slot], att_ss.at[n], att_rs.at[slot], (dap, qs[n]))

    for n in range(1, SEQ):
        att_copy(n, seq).start()
    att_ref[seq] = att_send[seq]

    each(zh + 1, ZH, pass_left)
    for py in range(Y):
        right_arrived(py * 2 + 1 - l)

    def left_of_core(px, pzh):
        slot = left_slot(1 - c, px, pzh)
        ref = left_all.at[slot]
        copy_to(ref, ref, left_ss.at[0], left_rs.at[slot], other_core).wait_recv()

    def tile_copy(plane, n):
        return copy_to(
            tiles.at[plane * X + xs[n]], tiles_in.at[zh * SEQ + seq],
            tile_ss.at[plane * X + n], tile_rs.at[zh * SEQ + seq],
            (dap_of(xs[n], plane, y), x),
        )

    def is_own(plane):
        return jnp.logical_and(x == seq, zh == plane)

    def own_tile(plane):
        return pltpu.make_async_copy(
            tiles.at[plane * X + x], tiles_in.at[zh * SEQ + seq], tile_rs.at[zh * SEQ + seq])

    groups = PROJECTED_DIM // 4
    turns = RIGHTS // 4
    lane_block = lax.broadcasted_iota(jnp.int32, (groups * PLANE, 128), 1) // PROJECTED_DIM
    norm_cols = amino_rows[:RIGHTS, :] * count

    def multiply(plane):
        first = plane * PLANE
        lefts = left_all[first:first + PLANE].reshape(PLANE * PROJECTED_DIM, SEQS).astype(F32)
        for half in range(2):
            left_wide[plane, half] = lefts[:, half * 128:(half + 1) * 128]
        for k in range(4):
            left_k = jnp.concatenate(
                [jnp.concatenate(
                    [left_wide[plane, half, pl.ds(4 * g + k, PLANE, stride=PROJECTED_DIM), :]
                     for half in range(2)], axis=1)
                 for g in range(groups)], axis=0).astype(BF16)
            blocks = [right_all[4 * turn + (m - k) % 4] for turn in range(turns) for m in range(4)]
            outer[plane, k] = dot_t(left_k, jnp.concatenate(blocks, axis=0))
        for a in range(4):
            flat = []
            for turn in range(turns):
                cols = slice(turn * 128, (turn + 1) * 128)
                chosen = outer[plane, (3 - a) % 4, :, cols]
                for m in range(3):
                    chosen = jnp.where(lane_block == m, outer[plane, (m - a) % 4, :, cols], chosen)
                flat.append(jnp.concatenate(
                    [chosen[g * PLANE:(g + 1) * PLANE] for g in range(groups)], axis=1))
            rows_a = jnp.concatenate(
                [couple[(4 * g + (m - a) % 4) * PROJECTED_DIM:(4 * g + (m - a) % 4 + 1) * PROJECTED_DIM, :]
                 for g in range(groups) for m in range(4)], axis=0)
            result = dot(jnp.concatenate(flat, axis=0).astype(BF16), rows_a)
            for turn in range(turns):
                at = (turn * 4 + a) * PLANE
                projected[plane, at:at + PLANE, :] = result[turn * PLANE:(turn + 1) * PLANE]
        for n in range(PLANE):
            i = RIGHTS + first + n
            norm = jnp.maximum(norm_cols * amino_rows[i:i + 1, :], 1.0)
            tiles[plane * X + n % X, n // X] = (
                projected[plane, pl.ds(n, RIGHTS, stride=PLANE), :] / norm).astype(BF16)

    for plane in range(ZH):
        pl.when(zh < plane)(functools.partial(take_left, plane))
        for px in range(X):
            left_of_core(px, plane)
        multiply(plane)
        for n in (1, 3, 2):
            tile_copy(plane, n).start()
        pl.when(jnp.logical_not(is_own(plane)))(lambda: tile_copy(plane, 0).start())
        pl.when(is_own(plane))(lambda: own_tile(plane).start())

    for n in range(1, SEQ):
        att_copy(n, qs[n]).wait_recv()

    for pzh in range(ZH):
        for pseq in range(SEQ):
            slot = pzh * SEQ + pseq
            pltpu.make_async_copy(tiles.at[0], tiles_in.at[slot], tile_rs.at[slot]).wait()
            for row in range(2):
                at = (pseq // 2 * 2 + row) * TILES * 8 + pzh * RIGHTS * 2 + pseq % 2
                pair_wide[pl.ds(at, RIGHTS, stride=2), :] = tiles_in[slot, row].astype(F32)
    pair_ref[...] = pair_wide[...].reshape(SEQ, TILES * 8, PAIR).astype(BF16)

    for n in range(1, SEQ):
        stack_copy(n, seq).wait_send()
        att_copy(n, seq).wait_send()
    for n in range(1, ZH):
        along_z(zs[n]).wait_send()
    for pzh in range(ZH):
        for n in range(1, X):
            along_x(pzh, n).wait_send()
        for px in range(X):
            to_core(px, pzh).wait_send()
    for copy in right_sent:
        copy.wait_send()
    for plane in range(ZH):
        for n in range(1, X):
            tile_copy(plane, n).wait_send()
        pl.when(jnp.logical_not(is_own(plane)))(lambda: tile_copy(plane, 0).wait_send())


def on_device(
    homolog_stack,
    homolog_existing_flags,
    amino_existing_flags,
    asking_weights,
    lookup_weights,
    content_weights,
    sigmoid_weights,
    final_projection,
    former_weights,
    latter_weights,
    couple_projection,
):
    block = SEQS // SEQ
    vmem = pl.BlockSpec(memory_space=pltpu.VMEM)
    hbm = pl.BlockSpec(memory_space=pltpu.HBM)
    dma = pltpu.SemaphoreType.DMA
    operands = (
        homolog_stack,
        homolog_existing_flags[None, :],
        amino_existing_flags[None, :],
        asking_weights, lookup_weights, content_weights, sigmoid_weights, final_projection,
        former_weights.T, latter_weights.T, couple_projection,
    )
    attended, pair = pl.pallas_call(
        kernel,
        out_shape=(
            pltpu.VMEM((SEQ, block, FEATURES), BF16),
            pltpu.VMEM((SEQ, TILES * 8, PAIR), BF16),
        ),
        in_specs=[hbm] * len(operands),
        out_specs=(vmem, vmem),
        scratch_shapes=[pltpu.VMEM(a.shape, a.dtype) for a in operands] + [
            dma((len(operands),)),
            pltpu.VMEM((SEQ, block, FEATURES), BF16),
            pltpu.VMEM((SEQ, block, FEATURES), BF16),
            pltpu.VMEM((SEQ, block, FEATURES), BF16),
            pltpu.VMEM((LEFTS, PROJECTED_DIM, SEQS), BF16),
            pltpu.VMEM((RIGHTS, PROJECTED_DIM, SEQS), BF16),
            pltpu.VMEM((4 * FEATURES, FEATURES), BF16),
            pltpu.VMEM((FEATURES, FEATURES), BF16),
            pltpu.VMEM((2 * PROJECTED_DIM, FEATURES), BF16),
            pltpu.VMEM((PROJECTED_DIM * PROJECTED_DIM, PAIR), BF16),
            pltpu.VMEM((SEQS, SEQS), F32),
            pltpu.VMEM((ZH, 2, PLANE * PROJECTED_DIM, SEQS // 2), F32),
            pltpu.VMEM((ZH, 4, PROJECTED_DIM // 4 * PLANE, RIGHTS * PROJECTED_DIM), F32),
            pltpu.VMEM((ZH, RIGHTS * PLANE, PAIR), F32),
            pltpu.VMEM((TILES, 2, RIGHTS, PAIR), BF16),
            pltpu.VMEM((TILES, 2, RIGHTS, PAIR), BF16),
            pltpu.VMEM((SEQ * TILES * 8, PAIR), F32),
            pltpu.VMEM((ROWS_PICKED, PAIR), F32),
            pltpu.SemaphoreType.REGULAR((ZH,)),
            dma((SEQ,)), dma((SEQ,)), dma((SEQ,)), dma((SEQ,)),
            dma((ZH + 2 * TILES,)), dma((LEFTS,)),
            dma((RIGHTS,)), dma((RIGHTS,)),
            dma((TILES,)), dma((ZH * SEQ,)),
        ],
        compiler_params=pltpu.CompilerParams(
            collective_id=0, has_side_effects=True, vmem_limit_bytes=60 * 2**20
        ),
        name="column_attention_outer_product",
    )(*operands)
    return attended.transpose(1, 0, 2), pair


def solution(mesh):
    in_specs = (P("seq", "dap", None), P(), P(), P(), P(), P(), P(), P(), P(), P(), P())
    out_specs = (P("seq", "dap", None), P("dap", "seq", None))
    return jax.shard_map(
        on_device, mesh=mesh, in_specs=in_specs, out_specs=out_specs, check_vma=False
    )
```

```python
import functools

import jax
import jax.numpy as jnp
from jax import lax
from jax.experimental import pallas as pl
from jax.experimental.pallas import tpu as pltpu
from jax.sharding import PartitionSpec as P

HEADS = 8
PER_HEAD_DIM = 32
PROJECTED_DIM = 32
PAIR = 128
FEATURES = 256
SEQS = 256
X, ZH, Y, SEQ = 4, 4, 8, 4
ROWS_PICKED = 64
LEFTS = X * ZH * 2
RIGHTS = Y * 2
PLANE = X * 2
TILES = X * ZH
MESH = pl.DeviceIdType.MESH
F32 = jnp.float32
BF16 = jnp.bfloat16


def dot(a, b):
    return lax.dot_general(a, b, (((1,), (0,)), ((), ())), preferred_element_type=F32)


def dot_t(a, b):
    return lax.dot_general(a, b, (((1,), (1,)), ((), ())), preferred_element_type=F32)


def eye(size):
    rows = lax.broadcasted_iota(jnp.int32, (size, size), 0)
    cols = lax.broadcasted_iota(jnp.int32, (size, size), 1)
    return jnp.where(rows == cols, 1.0, 0.0).astype(BF16)


def rescale(values, axis):
    mean = jnp.mean(values, axis=axis, keepdims=True)
    centred = values - mean
    variance = jnp.mean(centred * centred, axis=axis, keepdims=True)
    return centred * lax.rsqrt(variance + 1e-05)


def kernel(
    stack_hbm, homolog_hbm, amino_hbm, asking_hbm, lookup_hbm, content_hbm, sigmoid_hbm, final_hbm,
    former_hbm, latter_hbm, couple_hbm,
    att_ref, pair_ref,
    stack_ref, homolog_ref, amino_ref, asking_ref, lookup_ref, content_ref, sigmoid_ref, final_ref,
    former_ref, latter_ref, couple_ref, local_sems,
    stack_send, stack_all, att_send, left_all, right_all, wt, wt_final, wt_pair, couple, key_mask,
    left_wide, outer, projected, tiles, tiles_in, pair_wide, amino_rows,
    here_sems, here_x, here_y, stack_ss, stack_rs, att_ss, att_rs, left_ss, left_rs,
    right_ss, right_rs, tile_ss, tile_rs,
):
    dap = lax.axis_index("dap")
    seq = lax.axis_index("seq")
    x, zh, y = lax.div(dap, ZH * Y), lax.rem(lax.div(dap, Y), ZH), lax.rem(dap, Y)
    l, c = lax.div(seq, 2), lax.rem(seq, 2)

    def dap_of(px, pzh, py):
        return (px * ZH + pzh) * Y + py

    xs = [x] + [lax.rem(x + n, X) for n in range(1, X)]
    zs = [zh] + [lax.rem(zh + n, ZH) for n in range(1, ZH)]
    ys = [y] + [lax.rem(y + n, Y) for n in range(1, Y)]
    qs = [seq] + [lax.rem(seq + n, SEQ) for n in range(1, SEQ)]

    def copy_to(src, dst, send_sem, recv_sem, device):
        return pltpu.make_async_remote_copy(
            src_ref=src, dst_ref=dst, send_sem=send_sem, recv_sem=recv_sem,
            device_id=device, device_id_type=MESH,
        )

    def each(lo, hi, body):
        def step(n, carry):
            body(n)
            return carry
        lax.fori_loop(lo, hi, step, 0)

    local_copies = [
        pltpu.make_async_copy(src, dst, local_sems.at[n])
        for n, (src, dst) in enumerate((
            (stack_hbm, stack_ref), (asking_hbm, asking_ref), (lookup_hbm, lookup_ref),
            (content_hbm, content_ref), (sigmoid_hbm, sigmoid_ref), (final_hbm, final_ref),
            (former_hbm, former_ref), (latter_hbm, latter_ref), (homolog_hbm, homolog_ref),
            (amino_hbm, amino_ref), (couple_hbm, couple_ref),
        ))
    ]
    local_copies[0].start()

    barrier = pltpu.get_barrier_semaphore()

    def greet(device):
        pl.semaphore_signal(barrier, inc=1, device_id=device, device_id_type=MESH)

    for q in qs[1:]:
        greet((dap, q))
    def from_first(py):
        return jnp.minimum(py, Y - py)

    here = from_first(y)
    for py in ys[1:]:
        pl.when(from_first(py) >= here)(lambda: greet((dap_of(x, zh, py), seq)))
    each(x + 1, X, lambda px: greet((dap_of(px, zh, y), seq)))
    each(zh + 1, ZH, lambda pzh: greet((dap_of(x, pzh, y), seq)))
    for copy in local_copies[1:]:
        copy.start()

    rows = lax.broadcasted_iota(jnp.int32, (SEQS, SEQS), 0)
    cols = lax.broadcasted_iota(jnp.int32, (SEQS, SEQS), 1)
    block = SEQS // SEQ
    by_residue = jnp.where(cols == rows % block * SEQ + rows // block, 1.0, 0.0).astype(BF16)
    local_copies[0].wait()
    stack_send[...] = dot(by_residue, stack_ref[...].reshape(SEQS, FEATURES)).astype(BF16).reshape(
        SEQ, block, FEATURES)

    pl.semaphore_wait(barrier, SEQ - 1 + x + 2 * here - lax.div(here, Y // 2) + zh)

    def stack_copy(n, slot):
        return copy_to(
            stack_send.at[qs[n]], stack_all.at[slot], stack_ss.at[n], stack_rs.at[slot], (dap, qs[n]))

    for n in range(1, SEQ):
        stack_copy(n, seq).start()

    def answer(pzh):
        pl.semaphore_signal(
            here_sems.at[zh], inc=1, device_id=(dap_of(x, pzh, y), seq), device_id_type=MESH)

    each(0, zh, answer)

    def answer_y(py):
        pl.semaphore_signal(
            here_y.at[y], inc=1, device_id=(dap_of(x, zh, py), seq), device_id_type=MESH)

    def answer_x(px):
        pl.semaphore_signal(
            here_x.at[x], inc=1, device_id=(dap_of(px, zh, y), seq), device_id_type=MESH)

    for py in ys[1:]:
        pl.when(from_first(py) < here)(functools.partial(answer_y, py))
    each(0, x, answer_x)
    stack_all[seq] = stack_send[seq]

    for copy in local_copies[1:]:
        copy.wait()
    ident = eye(FEATURES)
    for n, ref in enumerate((asking_ref, content_ref, sigmoid_ref)):
        wt[n * FEATURES:(n + 1) * FEATURES, :] = dot_t(ident, ref[...]).astype(BF16)
    wt_final[...] = dot_t(ident, final_ref[...]).astype(BF16)
    wt_pair[:PROJECTED_DIM, :] = former_ref[...]
    wt_pair[PROJECTED_DIM:, :] = latter_ref[...]
    couple[...] = couple_ref[...].astype(BF16)
    flags = homolog_ref[...].astype(F32)
    diagonal = (ident.astype(F32) * flags).astype(BF16)
    key_mask[...] = dot(diagonal, jnp.ones((SEQS, SEQS), BF16))
    count = jnp.sum(flags, axis=1, keepdims=True)
    residues = amino_ref.shape[1]
    shape = (ROWS_PICKED, residues)
    rows = lax.broadcasted_iota(jnp.int32, shape, 0)
    cols = lax.broadcasted_iota(jnp.int32, shape, 1)
    wanted = jnp.where(
        rows < RIGHTS, dap_of(x, zh, 0) * SEQ + 2 * rows + c,
        jnp.where(
            rows < RIGHTS + LEFTS,
            dap_of((rows - RIGHTS) % X, (rows - RIGHTS) // PLANE, y) * SEQ + 2 * l
            + (rows - RIGHTS) // X % 2,
            dap * SEQ + seq,
        ),
    )
    picked = jnp.where(cols == wanted, 1.0, 0.0).astype(BF16)
    amino_wide = jnp.broadcast_to(amino_ref[...].astype(F32), (PAIR, residues)).astype(BF16)
    amino_rows[...] = dot_t(picked, amino_wide)

    for n in range(1, SEQ):
        stack_copy(n, qs[n]).wait_recv()

    stack = stack_all[...].reshape(SEQS, FEATURES)
    normed = rescale(stack.astype(F32), 1).astype(BF16)
    query = (dot_t(wt[0:256, :], normed) * PER_HEAD_DIM ** (-0.5)).astype(BF16)
    key = dot(normed, lookup_ref[...]).astype(BF16)
    value = dot_t(wt[256:512, :], normed).astype(BF16)
    gate = jax.nn.sigmoid(dot_t(wt[512:768, :], normed))
    incoming = dot_t(ident, stack)
    unmasked = key_mask[...] > 0.5
    gated = []
    for h in range(HEADS):
        lo = h * PER_HEAD_DIM
        group = lo // 128 * 128
        before, after = lo - group, 128 - PER_HEAD_DIM - (lo - group)
        parts = [query[lo:lo + PER_HEAD_DIM]]
        if before:
            parts.insert(0, jnp.zeros((before, SEQS), BF16))
        if after:
            parts.append(jnp.zeros((after, SEQS), BF16))
        scores = dot(key[:, group:group + 128], jnp.concatenate(parts, axis=0))
        scores = jnp.where(unmasked, scores, -1000000000.0)
        weights = jnp.exp(scores - jnp.max(scores, axis=0, keepdims=True))
        total = jnp.sum(weights, axis=0, keepdims=True)
        mixed = dot(value[lo:lo + PER_HEAD_DIM], weights.astype(BF16))
        gated.append((gate[lo:lo + PER_HEAD_DIM] * (mixed / total)).astype(BF16))
    gated = jnp.concatenate(gated, axis=0)
    attended = (incoming + dot(wt_final[...], gated)).astype(BF16)

    amino_here = amino_rows[RIGHTS + LEFTS:RIGHTS + LEFTS + 1, :]
    normed2 = rescale(attended.astype(F32), 0).astype(BF16)
    sides = (dot(wt_pair[...], normed2) * (flags * jnp.concatenate([amino_here, amino_here], axis=1))).astype(BF16)

    def right_copy(slot, send_sem, device):
        ref = right_all.at[slot]
        return copy_to(ref, ref, send_sem, right_rs.at[slot], device)

    def right_arrived(slot):
        right_copy(slot, right_ss.at[0], (dap, qs[1])).wait_recv()

    other_l = (dap, (1 - l) * 2 + c)
    other_core = (dap, l * 2 + 1 - c)
    right_sent = []

    def send_right(slot, device):
        copy = right_copy(slot, right_ss.at[len(right_sent)], device)
        copy.start()
        right_sent.append(copy)

    own = y * 2 + l

    def left_slot(core, px, pzh):
        return pzh * PLANE + core * X + px

    def left_copy(px, pzh, n, device):
        slot = left_slot(c, px, pzh)
        return copy_to(left_all.at[slot], left_all.at[slot], left_ss.at[n], left_rs.at[slot], device)

    def along_z(pzh):
        return left_copy(x, zh, pzh, (dap_of(x, pzh, y), seq))

    def along_x(pzh, n):
        return left_copy(x, pzh, ZH + pzh * X + n, (dap_of(xs[n], zh, y), seq))

    def to_core(px, pzh):
        return left_copy(px, pzh, ZH + TILES + px * ZH + pzh, other_core)

    def spread(pzh):
        for n in (1, 3, 2):
            along_x(pzh, n).start()
        to_core(x, pzh).start()

    def left_arrived(px, pzh):
        left_copy(px, pzh, 0, (dap, qs[1])).wait_recv()

    def pass_left(pzh):
        left_arrived(x, pzh)
        spread(pzh)

    def take_left(pzh):
        for n in (1, 3, 2):
            left_arrived(xs[n], pzh)
            to_core(xs[n], pzh).start()

    left_all[left_slot(c, x, zh)] = sides[:PROJECTED_DIM]
    each(0, zh, lambda pzh: along_z(pzh).start())
    right_all[own] = sides[PROJECTED_DIM:]
    send_right(own, other_l)
    for n in (4, 3, 5, 2, 6, 1, 7):
        pl.when(from_first(ys[n]) > here)(lambda: pl.semaphore_wait(here_y.at[ys[n]], 1))
        send_right(own, (dap_of(x, zh, ys[n]), seq))
    each(x + 1, X, lambda px: pl.semaphore_wait(here_x.at[px], 1))
    spread(zh)

    def send_above(pzh):
        pl.semaphore_wait(here_sems.at[pzh], 1)
        along_z(pzh).start()

    each(zh + 1, ZH, send_above)

    def pass_y(n):
        slot = ys[n] * 2 + l
        right_arrived(slot)
        send_right(slot, other_l)

    att_send[...] = dot_t(ident, attended).astype(BF16).reshape(SEQ, SEQS // SEQ, FEATURES)
    pass_y(1)
    pass_y(7)
    each(0, zh, pass_left)
    pass_y(2)
    pass_y(6)
    pass_y(3)
    pass_y(5)
    pass_y(4)
    each(0, jnp.minimum(zh + 1, ZH - 1), take_left)

    def att_copy(n, slot):
        return copy_to(
            att_send.at[qs[n]], att_ref.at[slot], att_ss.at[n], att_rs.at[slot], (dap, qs[n]))

    each(zh + 1, ZH, pass_left)
    for py in range(Y):
        right_arrived(py * 2 + 1 - l)

    def left_of_core(px, pzh):
        slot = left_slot(1 - c, px, pzh)
        ref = left_all.at[slot]
        copy_to(ref, ref, left_ss.at[0], left_rs.at[slot], other_core).wait_recv()

    def tile_copy(plane, n):
        return copy_to(
            tiles.at[plane * X + xs[n]], tiles_in.at[zh * SEQ + seq],
            tile_ss.at[plane * X + n], tile_rs.at[zh * SEQ + seq],
            (dap_of(xs[n], plane, y), x),
        )

    def is_own(plane):
        return jnp.logical_and(x == seq, zh == plane)

    def own_tile(plane):
        return pltpu.make_async_copy(
            tiles.at[plane * X + x], tiles_in.at[zh * SEQ + seq], tile_rs.at[zh * SEQ + seq])

    groups = PROJECTED_DIM // 4
    turns = RIGHTS // 4
    lane_block = lax.broadcasted_iota(jnp.int32, (groups * PLANE, 128), 1) // PROJECTED_DIM
    norm_cols = amino_rows[:RIGHTS, :] * count

    def multiply(plane):
        first = plane * PLANE
        lefts = left_all[first:first + PLANE].reshape(PLANE * PROJECTED_DIM, SEQS).astype(F32)
        for half in range(2):
            left_wide[plane, half] = lefts[:, half * 128:(half + 1) * 128]
        for k in range(4):
            left_k = jnp.concatenate(
                [jnp.concatenate(
                    [left_wide[plane, half, pl.ds(4 * g + k, PLANE, stride=PROJECTED_DIM), :]
                     for half in range(2)], axis=1)
                 for g in range(groups)], axis=0).astype(BF16)
            blocks = [right_all[4 * turn + (m - k) % 4] for turn in range(turns) for m in range(4)]
            outer[plane, k] = dot_t(left_k, jnp.concatenate(blocks, axis=0))
        for a in range(4):
            flat = []
            for turn in range(turns):
                cols = slice(turn * 128, (turn + 1) * 128)
                chosen = outer[plane, (3 - a) % 4, :, cols]
                for m in range(3):
                    chosen = jnp.where(lane_block == m, outer[plane, (m - a) % 4, :, cols], chosen)
                flat.append(jnp.concatenate(
                    [chosen[g * PLANE:(g + 1) * PLANE] for g in range(groups)], axis=1))
            rows_a = jnp.concatenate(
                [couple[(4 * g + (m - a) % 4) * PROJECTED_DIM:(4 * g + (m - a) % 4 + 1) * PROJECTED_DIM, :]
                 for g in range(groups) for m in range(4)], axis=0)
            result = dot(jnp.concatenate(flat, axis=0).astype(BF16), rows_a)
            for turn in range(turns):
                at = (turn * 4 + a) * PLANE
                projected[plane, at:at + PLANE, :] = result[turn * PLANE:(turn + 1) * PLANE]
        for n in range(PLANE):
            i = RIGHTS + first + n
            norm = jnp.maximum(norm_cols * amino_rows[i:i + 1, :], 1.0)
            tiles[plane * X + n % X, n // X] = (
                projected[plane, pl.ds(n, RIGHTS, stride=PLANE), :] / norm).astype(BF16)

    for plane in range(ZH):
        pl.when(jnp.logical_or(zh < plane, plane == ZH - 1))(functools.partial(take_left, plane))
        for px in range(X):
            left_of_core(px, plane)
        multiply(plane)
        for n in (1, 3, 2):
            tile_copy(plane, n).start()
        pl.when(jnp.logical_not(is_own(plane)))(lambda: tile_copy(plane, 0).start())
        pl.when(is_own(plane))(lambda: own_tile(plane).start())
        if plane == 0:
            for n in range(1, SEQ):
                att_copy(n, seq).start()
            att_ref[seq] = att_send[seq]

    for n in range(1, SEQ):
        att_copy(n, qs[n]).wait_recv()

    for pzh in range(ZH):
        for pseq in range(SEQ):
            slot = pzh * SEQ + pseq
            pltpu.make_async_copy(tiles.at[0], tiles_in.at[slot], tile_rs.at[slot]).wait()
            for row in range(2):
                at = (pseq // 2 * 2 + row) * TILES * 8 + pzh * RIGHTS * 2 + pseq % 2
                pair_wide[pl.ds(at, RIGHTS, stride=2), :] = tiles_in[slot, row].astype(F32)
    pair_ref[...] = pair_wide[...].reshape(SEQ, TILES * 8, PAIR).astype(BF16)

    for n in range(1, SEQ):
        stack_copy(n, seq).wait_send()
        att_copy(n, seq).wait_send()
    for n in range(1, ZH):
        along_z(zs[n]).wait_send()
    for pzh in range(ZH):
        for n in range(1, X):
            along_x(pzh, n).wait_send()
        for px in range(X):
            to_core(px, pzh).wait_send()
    for copy in right_sent:
        copy.wait_send()
    for plane in range(ZH):
        for n in range(1, X):
            tile_copy(plane, n).wait_send()
        pl.when(jnp.logical_not(is_own(plane)))(lambda: tile_copy(plane, 0).wait_send())


def on_device(
    homolog_stack,
    homolog_existing_flags,
    amino_existing_flags,
    asking_weights,
    lookup_weights,
    content_weights,
    sigmoid_weights,
    final_projection,
    former_weights,
    latter_weights,
    couple_projection,
):
    block = SEQS // SEQ
    vmem = pl.BlockSpec(memory_space=pltpu.VMEM)
    hbm = pl.BlockSpec(memory_space=pltpu.HBM)
    dma = pltpu.SemaphoreType.DMA
    operands = (
        homolog_stack,
        homolog_existing_flags[None, :],
        amino_existing_flags[None, :],
        asking_weights, lookup_weights, content_weights, sigmoid_weights, final_projection,
        former_weights.T, latter_weights.T, couple_projection,
    )
    attended, pair = pl.pallas_call(
        kernel,
        out_shape=(
            pltpu.VMEM((SEQ, block, FEATURES), BF16),
            pltpu.VMEM((SEQ, TILES * 8, PAIR), BF16),
        ),
        in_specs=[hbm] * len(operands),
        out_specs=(vmem, vmem),
        scratch_shapes=[pltpu.VMEM(a.shape, a.dtype) for a in operands] + [
            dma((len(operands),)),
            pltpu.VMEM((SEQ, block, FEATURES), BF16),
            pltpu.VMEM((SEQ, block, FEATURES), BF16),
            pltpu.VMEM((SEQ, block, FEATURES), BF16),
            pltpu.VMEM((LEFTS, PROJECTED_DIM, SEQS), BF16),
            pltpu.VMEM((RIGHTS, PROJECTED_DIM, SEQS), BF16),
            pltpu.VMEM((3 * FEATURES, FEATURES), BF16),
            pltpu.VMEM((FEATURES, FEATURES), BF16),
            pltpu.VMEM((2 * PROJECTED_DIM, FEATURES), BF16),
            pltpu.VMEM((PROJECTED_DIM * PROJECTED_DIM, PAIR), BF16),
            pltpu.VMEM((SEQS, SEQS), F32),
            pltpu.VMEM((ZH, 2, PLANE * PROJECTED_DIM, SEQS // 2), F32),
            pltpu.VMEM((ZH, 4, PROJECTED_DIM // 4 * PLANE, RIGHTS * PROJECTED_DIM), F32),
            pltpu.VMEM((ZH, RIGHTS * PLANE, PAIR), F32),
            pltpu.VMEM((TILES, 2, RIGHTS, PAIR), BF16),
            pltpu.VMEM((TILES, 2, RIGHTS, PAIR), BF16),
            pltpu.VMEM((SEQ * TILES * 8, PAIR), F32),
            pltpu.VMEM((ROWS_PICKED, PAIR), F32),
            pltpu.SemaphoreType.REGULAR((ZH,)), pltpu.SemaphoreType.REGULAR((X,)), pltpu.SemaphoreType.REGULAR((Y,)),
            dma((SEQ,)), dma((SEQ,)), dma((SEQ,)), dma((SEQ,)),
            dma((ZH + 2 * TILES,)), dma((LEFTS,)),
            dma((RIGHTS,)), dma((RIGHTS,)),
            dma((TILES,)), dma((ZH * SEQ,)),
        ],
        compiler_params=pltpu.CompilerParams(
            collective_id=0, has_side_effects=True, vmem_limit_bytes=60 * 2**20
        ),
        name="column_attention_outer_product",
    )(*operands)
    return attended.transpose(1, 0, 2), pair


def solution(mesh):
    in_specs = (P("seq", "dap", None), P(), P(), P(), P(), P(), P(), P(), P(), P(), P())
    out_specs = (P("seq", "dap", None), P("dap", "seq", None))
    return jax.shard_map(
        on_device, mesh=mesh, in_specs=in_specs, out_specs=out_specs, check_vma=False
    )
```

```python
import functools

import jax
import jax.numpy as jnp
from jax import lax
from jax.experimental import pallas as pl
from jax.experimental.pallas import tpu as pltpu
from jax.sharding import PartitionSpec as P

HEADS = 8
PER_HEAD_DIM = 32
PROJECTED_DIM = 32
PAIR = 128
FEATURES = 256
SEQS = 256
X, ZH, Y, SEQ = 4, 4, 8, 4
ROWS_PICKED = 64
LEFTS = X * ZH * 2
RIGHTS = Y * 2
PLANE = X * 2
TILES = X * ZH
MESH = pl.DeviceIdType.MESH
F32 = jnp.float32
BF16 = jnp.bfloat16


def dot(a, b):
    return lax.dot_general(a, b, (((1,), (0,)), ((), ())), preferred_element_type=F32)


def dot_t(a, b):
    return lax.dot_general(a, b, (((1,), (1,)), ((), ())), preferred_element_type=F32)


def eye(size):
    rows = lax.broadcasted_iota(jnp.int32, (size, size), 0)
    cols = lax.broadcasted_iota(jnp.int32, (size, size), 1)
    return jnp.where(rows == cols, 1.0, 0.0).astype(BF16)


def rescale(values, axis):
    mean = jnp.mean(values, axis=axis, keepdims=True)
    centred = values - mean
    variance = jnp.mean(centred * centred, axis=axis, keepdims=True)
    return centred * lax.rsqrt(variance + 1e-05)


def kernel(
    stack_hbm, homolog_hbm, amino_hbm, asking_hbm, lookup_hbm, content_hbm, sigmoid_hbm, final_hbm,
    former_hbm, latter_hbm, couple_hbm,
    att_ref, pair_ref,
    stack_ref, homolog_ref, amino_ref, asking_ref, lookup_ref, content_ref, sigmoid_ref, final_ref,
    former_ref, latter_ref, couple_ref, local_sems,
    stack_send, stack_all, att_send, left_all, right_all, wt, wt_final, wt_pair, couple, key_mask,
    left_wide, outer, projected, tiles, tiles_in, pair_wide, amino_rows,
    here_sems, here_x, here_y, stack_ss, stack_rs, att_ss, att_rs, left_ss, left_rs,
    right_ss, right_rs, tile_ss, tile_rs,
):
    dap = lax.axis_index("dap")
    seq = lax.axis_index("seq")
    x, zh, y = lax.div(dap, ZH * Y), lax.rem(lax.div(dap, Y), ZH), lax.rem(dap, Y)
    l, c = lax.div(seq, 2), lax.rem(seq, 2)

    def dap_of(px, pzh, py):
        return (px * ZH + pzh) * Y + py

    xs = [x] + [lax.rem(x + n, X) for n in range(1, X)]
    zs = [zh] + [lax.rem(zh + n, ZH) for n in range(1, ZH)]
    ys = [y] + [lax.rem(y + n, Y) for n in range(1, Y)]
    qs = [seq] + [lax.rem(seq + n, SEQ) for n in range(1, SEQ)]

    def copy_to(src, dst, send_sem, recv_sem, device):
        return pltpu.make_async_remote_copy(
            src_ref=src, dst_ref=dst, send_sem=send_sem, recv_sem=recv_sem,
            device_id=device, device_id_type=MESH,
        )

    def each(lo, hi, body):
        def step(n, carry):
            body(n)
            return carry
        lax.fori_loop(lo, hi, step, 0)

    local_copies = [
        pltpu.make_async_copy(src, dst, local_sems.at[n])
        for n, (src, dst) in enumerate((
            (stack_hbm, stack_ref), (asking_hbm, asking_ref), (lookup_hbm, lookup_ref),
            (content_hbm, content_ref), (sigmoid_hbm, sigmoid_ref), (final_hbm, final_ref),
            (former_hbm, former_ref), (latter_hbm, latter_ref), (homolog_hbm, homolog_ref),
            (amino_hbm, amino_ref), (couple_hbm, couple_ref),
        ))
    ]
    local_copies[0].start()

    barrier = pltpu.get_barrier_semaphore()

    def greet(device):
        pl.semaphore_signal(barrier, inc=1, device_id=device, device_id_type=MESH)

    for q in qs[1:]:
        greet((dap, q))
    def from_first(py):
        return jnp.minimum(py, Y - py)

    here = from_first(y)
    for py in ys[1:]:
        pl.when(from_first(py) >= here)(lambda: greet((dap_of(x, zh, py), seq)))
    each(x + 1, X, lambda px: greet((dap_of(px, zh, y), seq)))
    each(zh + 1, ZH, lambda pzh: greet((dap_of(x, pzh, y), seq)))
    for copy in local_copies[1:]:
        copy.start()

    rows = lax.broadcasted_iota(jnp.int32, (SEQS, SEQS), 0)
    cols = lax.broadcasted_iota(jnp.int32, (SEQS, SEQS), 1)
    block = SEQS // SEQ
    by_residue = jnp.where(cols == rows % block * SEQ + rows // block, 1.0, 0.0).astype(BF16)
    local_copies[0].wait()
    stack_send[...] = dot(by_residue, stack_ref[...].reshape(SEQS, FEATURES)).astype(BF16).reshape(
        SEQ, block, FEATURES)

    pl.semaphore_wait(barrier, SEQ - 1 + x + 2 * here - lax.div(here, Y // 2) + zh)

    def stack_copy(n, slot):
        return copy_to(
            stack_send.at[qs[n]], stack_all.at[slot], stack_ss.at[n], stack_rs.at[slot], (dap, qs[n]))

    for n in range(1, SEQ):
        stack_copy(n, seq).start()

    def answer(pzh):
        pl.semaphore_signal(
            here_sems.at[zh], inc=1, device_id=(dap_of(x, pzh, y), seq), device_id_type=MESH)

    each(0, zh, answer)

    def answer_y(py):
        pl.semaphore_signal(
            here_y.at[y], inc=1, device_id=(dap_of(x, zh, py), seq), device_id_type=MESH)

    def answer_x(px):
        pl.semaphore_signal(
            here_x.at[x], inc=1, device_id=(dap_of(px, zh, y), seq), device_id_type=MESH)

    for py in ys[1:]:
        pl.when(from_first(py) < here)(functools.partial(answer_y, py))
    each(0, x, answer_x)
    stack_all[seq] = stack_send[seq]

    for copy in local_copies[1:]:
        copy.wait()
    ident = eye(FEATURES)
    for n, ref in enumerate((asking_ref, content_ref, sigmoid_ref)):
        wt[n * FEATURES:(n + 1) * FEATURES, :] = dot_t(ident, ref[...]).astype(BF16)
    wt_final[...] = dot_t(ident, final_ref[...]).astype(BF16)
    wt_pair[:PROJECTED_DIM, :] = former_ref[...]
    wt_pair[PROJECTED_DIM:, :] = latter_ref[...]
    couple[...] = couple_ref[...].astype(BF16)
    flags = homolog_ref[...].astype(F32)
    diagonal = (ident.astype(F32) * flags).astype(BF16)
    key_mask[...] = dot(diagonal, jnp.ones((SEQS, SEQS), BF16))
    count = jnp.sum(flags, axis=1, keepdims=True)
    residues = amino_ref.shape[1]
    shape = (ROWS_PICKED, residues)
    rows = lax.broadcasted_iota(jnp.int32, shape, 0)
    cols = lax.broadcasted_iota(jnp.int32, shape, 1)
    wanted = jnp.where(
        rows < RIGHTS, dap_of(x, zh, 0) * SEQ + 2 * rows + c,
        jnp.where(
            rows < RIGHTS + LEFTS,
            dap_of((rows - RIGHTS) % X, (rows - RIGHTS) // PLANE, y) * SEQ + 2 * l
            + (rows - RIGHTS) // X % 2,
            dap * SEQ + seq,
        ),
    )
    picked = jnp.where(cols == wanted, 1.0, 0.0).astype(BF16)
    amino_wide = jnp.broadcast_to(amino_ref[...].astype(F32), (PAIR, residues)).astype(BF16)
    amino_rows[...] = dot_t(picked, amino_wide)

    for n in range(1, SEQ):
        stack_copy(n, qs[n]).wait_recv()

    stack = stack_all[...].reshape(SEQS, FEATURES)
    normed = rescale(stack.astype(F32), 1).astype(BF16)
    query = (dot_t(wt[0:256, :], normed) * PER_HEAD_DIM ** (-0.5)).astype(BF16)
    key = dot(normed, lookup_ref[...]).astype(BF16)
    value = dot_t(wt[256:512, :], normed).astype(BF16)
    gate = jax.nn.sigmoid(dot_t(wt[512:768, :], normed))
    incoming = dot_t(ident, stack)
    unmasked = key_mask[...] > 0.5
    gated = []
    for h in range(HEADS):
        lo = h * PER_HEAD_DIM
        group = lo // 128 * 128
        before, after = lo - group, 128 - PER_HEAD_DIM - (lo - group)
        parts = [query[lo:lo + PER_HEAD_DIM]]
        if before:
            parts.insert(0, jnp.zeros((before, SEQS), BF16))
        if after:
            parts.append(jnp.zeros((after, SEQS), BF16))
        scores = dot(key[:, group:group + 128], jnp.concatenate(parts, axis=0))
        scores = jnp.where(unmasked, scores, -1000000000.0)
        weights = jnp.exp(scores - jnp.max(scores, axis=0, keepdims=True))
        total = jnp.sum(weights, axis=0, keepdims=True)
        mixed = dot(value[lo:lo + PER_HEAD_DIM], weights.astype(BF16))
        gated.append((gate[lo:lo + PER_HEAD_DIM] * (mixed / total)).astype(BF16))
    gated = jnp.concatenate(gated, axis=0)
    attended = (incoming + dot(wt_final[...], gated)).astype(BF16)

    amino_here = amino_rows[RIGHTS + LEFTS:RIGHTS + LEFTS + 1, :]
    normed2 = rescale(attended.astype(F32), 0).astype(BF16)
    sides = (dot(wt_pair[...], normed2) * (flags * jnp.concatenate([amino_here, amino_here], axis=1))).astype(BF16)

    def right_copy(slot, send_sem, device):
        ref = right_all.at[slot]
        return copy_to(ref, ref, send_sem, right_rs.at[slot], device)

    def right_arrived(slot):
        right_copy(slot, right_ss.at[0], (dap, qs[1])).wait_recv()

    other_l = (dap, (1 - l) * 2 + c)
    other_core = (dap, l * 2 + 1 - c)
    right_sent = []

    def send_right(slot, device):
        copy = right_copy(slot, right_ss.at[len(right_sent)], device)
        copy.start()
        right_sent.append(copy)

    own = y * 2 + l

    def left_slot(core, px, pzh):
        return pzh * PLANE + core * X + px

    def left_copy(px, pzh, n, device):
        slot = left_slot(c, px, pzh)
        return copy_to(left_all.at[slot], left_all.at[slot], left_ss.at[n], left_rs.at[slot], device)

    def along_z(pzh):
        return left_copy(x, zh, pzh, (dap_of(x, pzh, y), seq))

    def along_x(pzh, n):
        return left_copy(x, pzh, ZH + pzh * X + n, (dap_of(xs[n], zh, y), seq))

    def to_core(px, pzh):
        return left_copy(px, pzh, ZH + TILES + px * ZH + pzh, other_core)

    def spread(pzh):
        for n in (1, 3, 2):
            along_x(pzh, n).start()
        to_core(x, pzh).start()

    def left_arrived(px, pzh):
        left_copy(px, pzh, 0, (dap, qs[1])).wait_recv()

    def pass_left(pzh):
        left_arrived(x, pzh)
        spread(pzh)

    def take_left(pzh):
        for n in (1, 3, 2):
            left_arrived(xs[n], pzh)
            to_core(xs[n], pzh).start()

    left_all[left_slot(c, x, zh)] = sides[:PROJECTED_DIM]
    each(0, zh, lambda pzh: along_z(pzh).start())
    right_all[own] = sides[PROJECTED_DIM:]
    send_right(own, other_l)
    for n in (1, 7, 2, 6, 3, 5, 4):
        pl.when(from_first(ys[n]) > here)(lambda: pl.semaphore_wait(here_y.at[ys[n]], 1))
        send_right(own, (dap_of(x, zh, ys[n]), seq))
    each(x + 1, X, lambda px: pl.semaphore_wait(here_x.at[px], 1))
    spread(zh)
    each(0, zh, pass_left)

    def send_above(pzh):
        pl.semaphore_wait(here_sems.at[pzh], 1)
        along_z(pzh).start()

    each(zh + 1, ZH, send_above)

    def pass_y(n):
        slot = ys[n] * 2 + l
        right_arrived(slot)
        send_right(slot, other_l)

    att_send[...] = dot_t(ident, attended).astype(BF16).reshape(SEQ, SEQS // SEQ, FEATURES)
    pass_y(1)
    pass_y(7)
    pass_y(2)
    pass_y(6)
    pass_y(3)
    pass_y(5)
    pass_y(4)
    each(0, jnp.minimum(zh + 1, ZH - 1), take_left)

    def att_copy(n, slot):
        return copy_to(
            att_send.at[qs[n]], att_ref.at[slot], att_ss.at[n], att_rs.at[slot], (dap, qs[n]))

    each(zh + 1, ZH, pass_left)

    def left_of_core(px, pzh):
        slot = left_slot(1 - c, px, pzh)
        ref = left_all.at[slot]
        copy_to(ref, ref, left_ss.at[0], left_rs.at[slot], other_core).wait_recv()

    def tile_copy(plane, n):
        return copy_to(
            tiles.at[plane * X + xs[n]], tiles_in.at[zh * SEQ + seq],
            tile_ss.at[plane * X + n], tile_rs.at[zh * SEQ + seq],
            (dap_of(xs[n], plane, y), x),
        )

    def is_own(plane):
        return jnp.logical_and(x == seq, zh == plane)

    def own_tile(plane):
        return pltpu.make_async_copy(
            tiles.at[plane * X + x], tiles_in.at[zh * SEQ + seq], tile_rs.at[zh * SEQ + seq])

    groups = PROJECTED_DIM // 4
    turns = RIGHTS // 4
    lane_block = lax.broadcasted_iota(jnp.int32, (groups * PLANE, 128), 1) // PROJECTED_DIM
    norm_cols = amino_rows[:RIGHTS, :] * count

    def multiply(plane):
        first = plane * PLANE
        lefts = left_all[first:first + PLANE].reshape(PLANE * PROJECTED_DIM, SEQS).astype(F32)
        for half in range(2):
            left_wide[plane, half] = lefts[:, half * 128:(half + 1) * 128]
        turned = [
            jnp.concatenate(
                [jnp.concatenate(
                    [left_wide[plane, half, pl.ds(4 * g + k, PLANE, stride=PROJECTED_DIM), :]
                     for half in range(2)], axis=1)
                 for g in range(groups)], axis=0).astype(BF16)
            for k in range(4)
        ]
        if plane == 0:
            for py in range(Y):
                right_arrived(py * 2 + 1 - l)
        for k in range(4):
            blocks = [right_all[4 * turn + (m - k) % 4] for turn in range(turns) for m in range(4)]
            outer[plane, k] = dot_t(turned[k], jnp.concatenate(blocks, axis=0))
        flat = []
        for turn in range(turns):
            lanes = slice(turn * 128, (turn + 1) * 128)
            for a in range(4):
                chosen = outer[plane, (3 - a) % 4, :, lanes]
                for m in range(3):
                    chosen = jnp.where(lane_block == m, outer[plane, (m - a) % 4, :, lanes], chosen)
                if a:
                    chosen = pltpu.roll(chosen, 128 - a * PROJECTED_DIM, 1)
                flat.append(jnp.concatenate(
                    [chosen[g * PLANE:(g + 1) * PLANE] for g in range(groups)], axis=1))
        projected[plane] = dot(jnp.concatenate(flat, axis=0).astype(BF16), couple[...])
        for n in range(PLANE):
            i = RIGHTS + first + n
            norm = jnp.maximum(norm_cols * amino_rows[i:i + 1, :], 1.0)
            tiles[plane * X + n % X, n // X] = (
                projected[plane, pl.ds(n, RIGHTS, stride=PLANE), :] / norm).astype(BF16)

    for plane in range(ZH):
        pl.when(jnp.logical_or(zh < plane, plane == ZH - 1))(functools.partial(take_left, plane))
        for px in range(X):
            left_of_core(px, plane)
        multiply(plane)
        for n in (1, 3, 2):
            tile_copy(plane, n).start()
        pl.when(jnp.logical_not(is_own(plane)))(lambda: tile_copy(plane, 0).start())
        pl.when(is_own(plane))(lambda: own_tile(plane).start())
        if plane == 0:
            for n in range(1, SEQ):
                att_copy(n, seq).start()
            att_ref[seq] = att_send[seq]

    for n in range(1, SEQ):
        att_copy(n, qs[n]).wait_recv()

    for pzh in range(ZH):
        for pseq in range(SEQ):
            slot = pzh * SEQ + pseq
            pltpu.make_async_copy(tiles.at[0], tiles_in.at[slot], tile_rs.at[slot]).wait()
            for row in range(2):
                at = (pseq // 2 * 2 + row) * TILES * 8 + pzh * RIGHTS * 2 + pseq % 2
                pair_wide[pl.ds(at, RIGHTS, stride=2), :] = tiles_in[slot, row].astype(F32)
    pair_ref[...] = pair_wide[...].reshape(SEQ, TILES * 8, PAIR).astype(BF16)

    for n in range(1, SEQ):
        stack_copy(n, seq).wait_send()
        att_copy(n, seq).wait_send()
    for n in range(1, ZH):
        along_z(zs[n]).wait_send()
    for pzh in range(ZH):
        for n in range(1, X):
            along_x(pzh, n).wait_send()
        for px in range(X):
            to_core(px, pzh).wait_send()
    for copy in right_sent:
        copy.wait_send()
    for plane in range(ZH):
        for n in range(1, X):
            tile_copy(plane, n).wait_send()
        pl.when(jnp.logical_not(is_own(plane)))(lambda: tile_copy(plane, 0).wait_send())


def on_device(
    homolog_stack,
    homolog_existing_flags,
    amino_existing_flags,
    asking_weights,
    lookup_weights,
    content_weights,
    sigmoid_weights,
    final_projection,
    former_weights,
    latter_weights,
    couple_projection,
):
    block = SEQS // SEQ
    vmem = pl.BlockSpec(memory_space=pltpu.VMEM)
    hbm = pl.BlockSpec(memory_space=pltpu.HBM)
    dma = pltpu.SemaphoreType.DMA
    operands = (
        homolog_stack,
        homolog_existing_flags[None, :],
        amino_existing_flags[None, :],
        asking_weights, lookup_weights, content_weights, sigmoid_weights, final_projection,
        former_weights.T, latter_weights.T, couple_projection,
    )
    attended, pair = pl.pallas_call(
        kernel,
        out_shape=(
            pltpu.VMEM((SEQ, block, FEATURES), BF16),
            pltpu.VMEM((SEQ, TILES * 8, PAIR), BF16),
        ),
        in_specs=[hbm] * len(operands),
        out_specs=(vmem, vmem),
        scratch_shapes=[pltpu.VMEM(a.shape, a.dtype) for a in operands] + [
            dma((len(operands),)),
            pltpu.VMEM((SEQ, block, FEATURES), BF16),
            pltpu.VMEM((SEQ, block, FEATURES), BF16),
            pltpu.VMEM((SEQ, block, FEATURES), BF16),
            pltpu.VMEM((LEFTS, PROJECTED_DIM, SEQS), BF16),
            pltpu.VMEM((RIGHTS, PROJECTED_DIM, SEQS), BF16),
            pltpu.VMEM((3 * FEATURES, FEATURES), BF16),
            pltpu.VMEM((FEATURES, FEATURES), BF16),
            pltpu.VMEM((2 * PROJECTED_DIM, FEATURES), BF16),
            pltpu.VMEM((PROJECTED_DIM * PROJECTED_DIM, PAIR), BF16),
            pltpu.VMEM((SEQS, SEQS), F32),
            pltpu.VMEM((ZH, 2, PLANE * PROJECTED_DIM, SEQS // 2), F32),
            pltpu.VMEM((ZH, 4, PROJECTED_DIM // 4 * PLANE, RIGHTS * PROJECTED_DIM), F32),
            pltpu.VMEM((ZH, RIGHTS * PLANE, PAIR), F32),
            pltpu.VMEM((TILES, 2, RIGHTS, PAIR), BF16),
            pltpu.VMEM((TILES, 2, RIGHTS, PAIR), BF16),
            pltpu.VMEM((SEQ * TILES * 8, PAIR), F32),
            pltpu.VMEM((ROWS_PICKED, PAIR), F32),
            pltpu.SemaphoreType.REGULAR((ZH,)), pltpu.SemaphoreType.REGULAR((X,)), pltpu.SemaphoreType.REGULAR((Y,)),
            dma((SEQ,)), dma((SEQ,)), dma((SEQ,)), dma((SEQ,)),
            dma((ZH + 2 * TILES,)), dma((LEFTS,)),
            dma((RIGHTS,)), dma((RIGHTS,)),
            dma((TILES,)), dma((ZH * SEQ,)),
        ],
        compiler_params=pltpu.CompilerParams(
            collective_id=0, has_side_effects=True, vmem_limit_bytes=60 * 2**20
        ),
        name="column_attention_outer_product",
    )(*operands)
    return attended.transpose(1, 0, 2), pair


def solution(mesh):
    in_specs = (P("seq", "dap", None), P(), P(), P(), P(), P(), P(), P(), P(), P(), P())
    out_specs = (P("seq", "dap", None), P("dap", "seq", None))
    return jax.shard_map(
        on_device, mesh=mesh, in_specs=in_specs, out_specs=out_specs, check_vma=False
    )
```

```python
import functools

import jax
import jax.numpy as jnp
from jax import lax
from jax.experimental import pallas as pl
from jax.experimental.pallas import tpu as pltpu
from jax.sharding import PartitionSpec as P

HEADS = 8
PER_HEAD_DIM = 32
PROJECTED_DIM = 32
PAIR = 128
FEATURES = 256
SEQS = 256
X, ZH, Y, SEQ = 4, 4, 8, 4
ROWS_PICKED = 64
LEFTS = X * ZH * 2
RIGHTS = Y * 2
PLANE = X * 2
TILES = X * ZH
MESH = pl.DeviceIdType.MESH
F32 = jnp.float32
BF16 = jnp.bfloat16


def dot(a, b):
    return lax.dot_general(a, b, (((1,), (0,)), ((), ())), preferred_element_type=F32)


def dot_t(a, b):
    return lax.dot_general(a, b, (((1,), (1,)), ((), ())), preferred_element_type=F32)


def eye(size):
    rows = lax.broadcasted_iota(jnp.int32, (size, size), 0)
    cols = lax.broadcasted_iota(jnp.int32, (size, size), 1)
    return jnp.where(rows == cols, 1.0, 0.0).astype(BF16)


def rescale(values, axis):
    mean = jnp.mean(values, axis=axis, keepdims=True)
    centred = values - mean
    variance = jnp.mean(centred * centred, axis=axis, keepdims=True)
    return centred * lax.rsqrt(variance + 1e-05)


def kernel(
    stack_hbm, homolog_hbm, amino_hbm, asking_hbm, lookup_hbm, content_hbm, sigmoid_hbm, final_hbm,
    former_hbm, latter_hbm, couple_hbm,
    att_ref, pair_ref,
    stack_ref, homolog_ref, amino_ref, asking_ref, lookup_ref, content_ref, sigmoid_ref, final_ref,
    former_ref, latter_ref, couple_ref, local_sems,
    stack_send, stack_all, att_send, left_all, right_all, wt, wt_final, wt_pair, couple, key_mask,
    left_wide, outer, projected, tiles, tiles_in, pair_wide, amino_rows,
    here_sems, here_x, here_y, stack_ss, stack_rs, att_ss, att_rs, left_ss, left_rs,
    right_ss, right_rs, tile_ss, tile_rs,
):
    dap = lax.axis_index("dap")
    seq = lax.axis_index("seq")
    x, zh, y = lax.div(dap, ZH * Y), lax.rem(lax.div(dap, Y), ZH), lax.rem(dap, Y)
    l, c = lax.div(seq, 2), lax.rem(seq, 2)

    def dap_of(px, pzh, py):
        return (px * ZH + pzh) * Y + py

    xs = [x] + [lax.rem(x + n, X) for n in range(1, X)]
    zs = [zh] + [lax.rem(zh + n, ZH) for n in range(1, ZH)]
    ys = [y] + [lax.rem(y + n, Y) for n in range(1, Y)]
    qs = [seq] + [lax.rem(seq + n, SEQ) for n in range(1, SEQ)]

    def copy_to(src, dst, send_sem, recv_sem, device):
        return pltpu.make_async_remote_copy(
            src_ref=src, dst_ref=dst, send_sem=send_sem, recv_sem=recv_sem,
            device_id=device, device_id_type=MESH,
        )

    def each(lo, hi, body):
        def step(n, carry):
            body(n)
            return carry
        lax.fori_loop(lo, hi, step, 0)

    local_copies = [
        pltpu.make_async_copy(src, dst, local_sems.at[n])
        for n, (src, dst) in enumerate((
            (stack_hbm, stack_ref), (asking_hbm, asking_ref), (lookup_hbm, lookup_ref),
            (content_hbm, content_ref), (sigmoid_hbm, sigmoid_ref), (final_hbm, final_ref),
            (former_hbm, former_ref), (latter_hbm, latter_ref), (homolog_hbm, homolog_ref),
            (amino_hbm, amino_ref), (couple_hbm, couple_ref),
        ))
    ]
    local_copies[0].start()

    barrier = pltpu.get_barrier_semaphore()

    def greet(device):
        pl.semaphore_signal(barrier, inc=1, device_id=device, device_id_type=MESH)

    for q in qs[1:]:
        greet((dap, q))
    def from_first(py):
        return jnp.minimum(py, Y - py)

    here = from_first(y)
    for py in ys[1:]:
        pl.when(from_first(py) >= here)(lambda: greet((dap_of(x, zh, py), seq)))
    each(x + 1, X, lambda px: greet((dap_of(px, zh, y), seq)))
    each(zh + 1, ZH, lambda pzh: greet((dap_of(x, pzh, y), seq)))
    for copy in local_copies[1:]:
        copy.start()

    rows = lax.broadcasted_iota(jnp.int32, (SEQS, SEQS), 0)
    cols = lax.broadcasted_iota(jnp.int32, (SEQS, SEQS), 1)
    block = SEQS // SEQ
    by_residue = jnp.where(cols == rows % block * SEQ + rows // block, 1.0, 0.0).astype(BF16)
    local_copies[0].wait()
    stack_send[...] = dot(by_residue, stack_ref[...].reshape(SEQS, FEATURES)).astype(BF16).reshape(
        SEQ, block, FEATURES)

    pl.semaphore_wait(barrier, SEQ - 1 + x + 2 * here - lax.div(here, Y // 2) + zh)

    def stack_copy(n, slot):
        return copy_to(
            stack_send.at[qs[n]], stack_all.at[slot], stack_ss.at[n], stack_rs.at[slot], (dap, qs[n]))

    for n in range(1, SEQ):
        stack_copy(n, seq).start()

    def answer(pzh):
        pl.semaphore_signal(
            here_sems.at[zh], inc=1, device_id=(dap_of(x, pzh, y), seq), device_id_type=MESH)

    each(0, zh, answer)

    def answer_y(py):
        pl.semaphore_signal(
            here_y.at[y], inc=1, device_id=(dap_of(x, zh, py), seq), device_id_type=MESH)

    def answer_x(px):
        pl.semaphore_signal(
            here_x.at[x], inc=1, device_id=(dap_of(px, zh, y), seq), device_id_type=MESH)

    for py in ys[1:]:
        pl.when(from_first(py) < here)(functools.partial(answer_y, py))
    each(0, x, answer_x)
    stack_all[seq] = stack_send[seq]

    for copy in local_copies[1:]:
        copy.wait()
    ident = eye(FEATURES)
    for n, ref in enumerate((asking_ref, content_ref, sigmoid_ref)):
        wt[n * FEATURES:(n + 1) * FEATURES, :] = dot_t(ident, ref[...]).astype(BF16)
    wt_final[...] = dot_t(ident, final_ref[...]).astype(BF16)
    wt_pair[:PROJECTED_DIM, :] = former_ref[...]
    wt_pair[PROJECTED_DIM:, :] = latter_ref[...]
    couple[...] = couple_ref[...].astype(BF16)
    flags = homolog_ref[...].astype(F32)
    diagonal = (ident.astype(F32) * flags).astype(BF16)
    key_mask[...] = dot(diagonal, jnp.ones((SEQS, SEQS), BF16))
    count = jnp.sum(flags, axis=1, keepdims=True)
    residues = amino_ref.shape[1]
    shape = (ROWS_PICKED, residues)
    rows = lax.broadcasted_iota(jnp.int32, shape, 0)
    cols = lax.broadcasted_iota(jnp.int32, shape, 1)
    wanted = jnp.where(
        rows < RIGHTS, dap_of(x, zh, 0) * SEQ + 2 * rows + c,
        jnp.where(
            rows < RIGHTS + LEFTS,
            dap_of((rows - RIGHTS) % X, (rows - RIGHTS) // PLANE, y) * SEQ + 2 * l
            + (rows - RIGHTS) // X % 2,
            dap * SEQ + seq,
        ),
    )
    picked = jnp.where(cols == wanted, 1.0, 0.0).astype(BF16)
    amino_wide = jnp.broadcast_to(amino_ref[...].astype(F32), (PAIR, residues)).astype(BF16)
    amino_rows[...] = dot_t(picked, amino_wide)

    for n in range(1, SEQ):
        stack_copy(n, qs[n]).wait_recv()

    stack = stack_all[...].reshape(SEQS, FEATURES)
    normed = rescale(stack.astype(F32), 1).astype(BF16)
    query = (dot_t(wt[0:256, :], normed) * PER_HEAD_DIM ** (-0.5)).astype(BF16)
    key = dot(normed, lookup_ref[...]).astype(BF16)
    value = dot_t(wt[256:512, :], normed).astype(BF16)
    gate = jax.nn.sigmoid(dot_t(wt[512:768, :], normed))
    incoming = dot_t(ident, stack)
    unmasked = key_mask[...] > 0.5
    gated = []
    for h in range(HEADS):
        lo = h * PER_HEAD_DIM
        group = lo // 128 * 128
        before, after = lo - group, 128 - PER_HEAD_DIM - (lo - group)
        parts = [query[lo:lo + PER_HEAD_DIM]]
        if before:
            parts.insert(0, jnp.zeros((before, SEQS), BF16))
        if after:
            parts.append(jnp.zeros((after, SEQS), BF16))
        scores = dot(key[:, group:group + 128], jnp.concatenate(parts, axis=0))
        scores = jnp.where(unmasked, scores, -1000000000.0)
        weights = jnp.exp(scores - jnp.max(scores, axis=0, keepdims=True))
        total = jnp.sum(weights, axis=0, keepdims=True)
        mixed = dot(value[lo:lo + PER_HEAD_DIM], weights.astype(BF16))
        gated.append((gate[lo:lo + PER_HEAD_DIM] * (mixed / total)).astype(BF16))
    gated = jnp.concatenate(gated, axis=0)
    attended = (incoming + dot(wt_final[...], gated)).astype(BF16)

    amino_here = amino_rows[RIGHTS + LEFTS:RIGHTS + LEFTS + 1, :]
    normed2 = rescale(attended.astype(F32), 0).astype(BF16)
    sides = (dot(wt_pair[...], normed2) * (flags * jnp.concatenate([amino_here, amino_here], axis=1))).astype(BF16)

    def right_copy(slot, send_sem, device):
        ref = right_all.at[slot]
        return copy_to(ref, ref, send_sem, right_rs.at[slot], device)

    def right_arrived(slot):
        right_copy(slot, right_ss.at[0], (dap, qs[1])).wait_recv()

    other_l = (dap, (1 - l) * 2 + c)
    other_core = (dap, l * 2 + 1 - c)
    right_sent = []

    def send_right(slot, device):
        copy = right_copy(slot, right_ss.at[len(right_sent)], device)
        copy.start()
        right_sent.append(copy)

    own = y * 2 + l

    def left_slot(core, px, pzh):
        return pzh * PLANE + core * X + px

    def left_copy(px, pzh, n, device):
        slot = left_slot(c, px, pzh)
        return copy_to(left_all.at[slot], left_all.at[slot], left_ss.at[n], left_rs.at[slot], device)

    def along_z(pzh):
        return left_copy(x, zh, pzh, (dap_of(x, pzh, y), seq))

    def along_x(pzh, n):
        return left_copy(x, pzh, ZH + pzh * X + n, (dap_of(xs[n], zh, y), seq))

    def to_core(px, pzh):
        return left_copy(px, pzh, ZH + TILES + px * ZH + pzh, other_core)

    def spread(pzh):
        for n in (1, 3, 2):
            along_x(pzh, n).start()
        to_core(x, pzh).start()

    def left_arrived(px, pzh):
        left_copy(px, pzh, 0, (dap, qs[1])).wait_recv()

    def pass_left(pzh):
        left_arrived(x, pzh)
        spread(pzh)

    def take_left(pzh):
        for n in (1, 3, 2):
            left_arrived(xs[n], pzh)
            to_core(xs[n], pzh).start()

    left_all[left_slot(c, x, zh)] = sides[:PROJECTED_DIM]
    each(0, zh, lambda pzh: along_z(pzh).start())
    right_all[own] = sides[PROJECTED_DIM:]
    send_right(own, other_l)
    for n in (1, 7, 2, 6, 3, 5, 4):
        pl.when(from_first(ys[n]) > here)(lambda: pl.semaphore_wait(here_y.at[ys[n]], 1))
        send_right(own, (dap_of(x, zh, ys[n]), seq))
    each(x + 1, X, lambda px: pl.semaphore_wait(here_x.at[px], 1))
    each(0, zh, pass_left)
    spread(zh)

    def send_above(pzh):
        pl.semaphore_wait(here_sems.at[pzh], 1)
        along_z(pzh).start()

    each(zh + 1, ZH, send_above)

    def pass_y(n):
        slot = ys[n] * 2 + l
        right_arrived(slot)
        send_right(slot, other_l)

    att_send[...] = dot_t(ident, attended).astype(BF16).reshape(SEQ, SEQS // SEQ, FEATURES)
    pass_y(1)
    pass_y(7)
    pass_y(2)
    pass_y(6)
    pass_y(3)
    pass_y(5)
    pass_y(4)
    each(0, jnp.minimum(zh + 1, ZH - 1), take_left)

    def att_copy(n, slot):
        return copy_to(
            att_send.at[qs[n]], att_ref.at[slot], att_ss.at[n], att_rs.at[slot], (dap, qs[n]))

    each(zh + 1, ZH, pass_left)

    def left_of_core(px, pzh):
        slot = left_slot(1 - c, px, pzh)
        ref = left_all.at[slot]
        copy_to(ref, ref, left_ss.at[0], left_rs.at[slot], other_core).wait_recv()

    def tile_copy(plane, n):
        return copy_to(
            tiles.at[plane * X + xs[n]], tiles_in.at[zh * SEQ + seq],
            tile_ss.at[plane * X + n], tile_rs.at[zh * SEQ + seq],
            (dap_of(xs[n], plane, y), x),
        )

    def is_own(plane):
        return jnp.logical_and(x == seq, zh == plane)

    def own_tile(plane):
        return pltpu.make_async_copy(
            tiles.at[plane * X + x], tiles_in.at[zh * SEQ + seq], tile_rs.at[zh * SEQ + seq])

    groups = PROJECTED_DIM // 4
    turns = RIGHTS // 4
    lane_block = lax.broadcasted_iota(jnp.int32, (groups * PLANE, 128), 1) // PROJECTED_DIM
    norm_cols = amino_rows[:RIGHTS, :] * count

    def multiply(plane):
        first = plane * PLANE
        lefts = left_all[first:first + PLANE].reshape(PLANE * PROJECTED_DIM, SEQS).astype(F32)
        for half in range(2):
            left_wide[plane, half] = lefts[:, half * 128:(half + 1) * 128]
        turned = [
            jnp.concatenate(
                [jnp.concatenate(
                    [left_wide[plane, half, pl.ds(4 * g + k, PLANE, stride=PROJECTED_DIM), :]
                     for half in range(2)], axis=1)
                 for g in range(groups)], axis=0).astype(BF16)
            for k in range(4)
        ]
        if plane == 0:
            for py in range(Y):
                right_arrived(py * 2 + 1 - l)
        for k in range(4):
            blocks = [right_all[4 * turn + (m - k) % 4] for turn in range(turns) for m in range(4)]
            outer[plane, k] = dot_t(turned[k], jnp.concatenate(blocks, axis=0))
        flat = []
        for turn in range(turns):
            lanes = slice(turn * 128, (turn + 1) * 128)
            for a in range(4):
                chosen = outer[plane, (3 - a) % 4, :, lanes]
                for m in range(3):
                    chosen = jnp.where(lane_block == m, outer[plane, (m - a) % 4, :, lanes], chosen)
                if a:
                    chosen = pltpu.roll(chosen, 128 - a * PROJECTED_DIM, 1)
                flat.append(jnp.concatenate(
                    [chosen[g * PLANE:(g + 1) * PLANE] for g in range(groups)], axis=1))
        projected[plane] = dot(jnp.concatenate(flat, axis=0).astype(BF16), couple[...])
        for n in range(PLANE):
            i = RIGHTS + first + n
            norm = jnp.maximum(norm_cols * amino_rows[i:i + 1, :], 1.0)
            tiles[plane * X + n % X, n // X] = (
                projected[plane, pl.ds(n, RIGHTS, stride=PLANE), :] / norm).astype(BF16)

    for plane in range(ZH):
        pl.when(jnp.logical_or(zh < plane, plane == ZH - 1))(functools.partial(take_left, plane))
        for px in range(X):
            left_of_core(px, plane)
        multiply(plane)
        for n in (1, 3, 2):
            tile_copy(plane, n).start()
        pl.when(jnp.logical_not(is_own(plane)))(lambda: tile_copy(plane, 0).start())
        pl.when(is_own(plane))(lambda: own_tile(plane).start())
        if plane == 0:
            for n in range(1, SEQ):
                att_copy(n, seq).start()
            att_ref[seq] = att_send[seq]

    for n in range(1, SEQ):
        att_copy(n, qs[n]).wait_recv()

    for pzh in range(ZH):
        for pseq in range(SEQ):
            slot = pzh * SEQ + pseq
            pltpu.make_async_copy(tiles.at[0], tiles_in.at[slot], tile_rs.at[slot]).wait()
            for row in range(2):
                at = (pseq // 2 * 2 + row) * TILES * 8 + pzh * RIGHTS * 2 + pseq % 2
                pair_wide[pl.ds(at, RIGHTS, stride=2), :] = tiles_in[slot, row].astype(F32)
    pair_ref[...] = pair_wide[...].reshape(SEQ, TILES * 8, PAIR).astype(BF16)

    for n in range(1, SEQ):
        stack_copy(n, seq).wait_send()
        att_copy(n, seq).wait_send()
    for n in range(1, ZH):
        along_z(zs[n]).wait_send()
    for pzh in range(ZH):
        for n in range(1, X):
            along_x(pzh, n).wait_send()
        for px in range(X):
            to_core(px, pzh).wait_send()
    for copy in right_sent:
        copy.wait_send()
    for plane in range(ZH):
        for n in range(1, X):
            tile_copy(plane, n).wait_send()
        pl.when(jnp.logical_not(is_own(plane)))(lambda: tile_copy(plane, 0).wait_send())


def on_device(
    homolog_stack,
    homolog_existing_flags,
    amino_existing_flags,
    asking_weights,
    lookup_weights,
    content_weights,
    sigmoid_weights,
    final_projection,
    former_weights,
    latter_weights,
    couple_projection,
):
    block = SEQS // SEQ
    vmem = pl.BlockSpec(memory_space=pltpu.VMEM)
    hbm = pl.BlockSpec(memory_space=pltpu.HBM)
    dma = pltpu.SemaphoreType.DMA
    operands = (
        homolog_stack,
        homolog_existing_flags[None, :],
        amino_existing_flags[None, :],
        asking_weights, lookup_weights, content_weights, sigmoid_weights, final_projection,
        former_weights.T, latter_weights.T, couple_projection,
    )
    attended, pair = pl.pallas_call(
        kernel,
        out_shape=(
            pltpu.VMEM((SEQ, block, FEATURES), BF16),
            pltpu.VMEM((SEQ, TILES * 8, PAIR), BF16),
        ),
        in_specs=[hbm] * len(operands),
        out_specs=(vmem, vmem),
        scratch_shapes=[pltpu.VMEM(a.shape, a.dtype) for a in operands] + [
            dma((len(operands),)),
            pltpu.VMEM((SEQ, block, FEATURES), BF16),
            pltpu.VMEM((SEQ, block, FEATURES), BF16),
            pltpu.VMEM((SEQ, block, FEATURES), BF16),
            pltpu.VMEM((LEFTS, PROJECTED_DIM, SEQS), BF16),
            pltpu.VMEM((RIGHTS, PROJECTED_DIM, SEQS), BF16),
            pltpu.VMEM((3 * FEATURES, FEATURES), BF16),
            pltpu.VMEM((FEATURES, FEATURES), BF16),
            pltpu.VMEM((2 * PROJECTED_DIM, FEATURES), BF16),
            pltpu.VMEM((PROJECTED_DIM * PROJECTED_DIM, PAIR), BF16),
            pltpu.VMEM((SEQS, SEQS), F32),
            pltpu.VMEM((ZH, 2, PLANE * PROJECTED_DIM, SEQS // 2), F32),
            pltpu.VMEM((ZH, 4, PROJECTED_DIM // 4 * PLANE, RIGHTS * PROJECTED_DIM), F32),
            pltpu.VMEM((ZH, RIGHTS * PLANE, PAIR), F32),
            pltpu.VMEM((TILES, 2, RIGHTS, PAIR), BF16),
            pltpu.VMEM((TILES, 2, RIGHTS, PAIR), BF16),
            pltpu.VMEM((SEQ * TILES * 8, PAIR), F32),
            pltpu.VMEM((ROWS_PICKED, PAIR), F32),
            pltpu.SemaphoreType.REGULAR((ZH,)), pltpu.SemaphoreType.REGULAR((X,)), pltpu.SemaphoreType.REGULAR((Y,)),
            dma((SEQ,)), dma((SEQ,)), dma((SEQ,)), dma((SEQ,)),
            dma((ZH + 2 * TILES,)), dma((LEFTS,)),
            dma((RIGHTS,)), dma((RIGHTS,)),
            dma((TILES,)), dma((ZH * SEQ,)),
        ],
        compiler_params=pltpu.CompilerParams(
            collective_id=0, has_side_effects=True, vmem_limit_bytes=60 * 2**20
        ),
        name="column_attention_outer_product",
    )(*operands)
    return attended.transpose(1, 0, 2), pair


def solution(mesh):
    in_specs = (P("seq", "dap", None), P(), P(), P(), P(), P(), P(), P(), P(), P(), P())
    out_specs = (P("seq", "dap", None), P("dap", "seq", None))
    return jax.shard_map(
        on_device, mesh=mesh, in_specs=in_specs, out_specs=out_specs, check_vma=False
    )
```
